512 devices in a mesh: dp: 16 (over z, y_hi), space: 32 (over x, y_lo, core).
Axes of the slice: x: 4, y: 8 (y_hi: 2, y_lo: 4; y = y_hi * 4 + y_lo), z: 8, core: 2. Of those that a mesh axis runs over, the one named last changes fastest.
Arguments:
- volume: bfloat16 [16, 4, 256, 8, 256], P('dp', None, 'space'), may hold values from -6 to 6
- first_weight: bfloat16 [32, 108], replicated, may hold values from -0.625 to 0.625
- first_bias: float32 [32], replicated, may hold values from -3 to 3
- second_weight: bfloat16 [64, 864], replicated, may hold values from -0.21875 to 0.21875
- second_bias: float32 [64], replicated, may hold values from -3 to 3
- cotangent: bfloat16 [16, 64, 128, 4, 128], P('dp', None, 'space'), may hold values from -6 to 6
Outputs:
- activation: bfloat16 [16, 64, 128, 4, 128], P('dp', None, 'space')
- grad_first_weight: float32 [32, 108], replicated
- grad_first_bias: float32 [32], replicated
- grad_second_weight: float32 [64, 864], replicated
- grad_second_bias: float32 [64], replicated
The draws below stay inside these ranges and needn't reach their ends.
All inputs are finite; a program needn't handle non-finite values.
Results may differ from the reference program's by a relative error of at most 0.011.
The reference program's roundings to bfloat16 on the way (of `pooled`, `grad_pre_second` and `grad_pre_first`) count: a program that leaves them out, or rounds other values in their place, can miss the bound.
Values may be sent and summed in bfloat16 or wider, within the bound.
No kernel may reach another device: no remote copies, remote signals or barrier semaphores. Data moves between devices by JAX's collectives and lax.ppermute only.
A program may use at most 128 MiB of HBM per device.

```python
import math
import jax
import jax.numpy as jnp
from jax import lax

C0 = 4
C1 = 32
C2 = 64
SY = 8
SZ = 256
BATCH = 16
NX = 256


def block_levels(key, shape, split, low, top_value):
    gain, own = 1.0, jax.random.fold_in(key, 6)
    for axis_at, blocks in split:
        heights = jnp.exp(jax.random.uniform(jax.random.fold_in(own, axis_at), (blocks,), jnp.float32, low / len(split), top_value / len(split)))
        gain = gain * jnp.repeat(heights, shape[axis_at] // blocks).reshape([-1 if axis == axis_at else 1 for axis in range(len(shape))])
    return gain


def gaussian(key, shape, deviation, bound, shards=(), kind=jnp.bfloat16):
    level = block_levels(key, shape, shards, -0.22, 0.18) if shards else 1.0
    entries = jax.random.normal(key, shape, jnp.float32) * deviation * level
    return jnp.minimum(jnp.maximum(entries, -bound), bound).astype(kind)


def setup_inputs(seed: int = 0) -> dict:
    arg_keys = jax.random.split(jax.random.key(seed), 7)
    volume = gaussian(arg_keys[0], (BATCH, C0, NX, SY, SZ), 1.0, 6.0, ((0, 16), (2, 32)))
    first_weight = gaussian(arg_keys[1], (C1, 27 * C0), (27 * C0) ** -0.5, 0.625)
    first_bias = gaussian(arg_keys[2], (C1,), 0.5, 3.0, (), jnp.float32)
    second_weight = gaussian(arg_keys[3], (C2, 27 * C1), (27 * C1) ** -0.5, 0.21875)
    second_bias = gaussian(arg_keys[4], (C2,), 0.5, 3.0, (), jnp.float32)
    cotangent = gaussian(arg_keys[5], (BATCH, C2, NX // 2, SY // 2, SZ // 2), 1.0, 6.0, ((0, 16), (2, 32)))
    return dict(volume=volume, first_weight=first_weight, first_bias=first_bias, second_weight=second_weight, second_bias=second_bias, cotangent=cotangent)


leak_slope = 0.3

def columns(padded, planes, height, depth):
    shifted = []
    for along_p in range(3):
        for along_y in range(3):
            for along_z in range(3):
                shifted.append(padded[:, along_p:along_p + planes, along_y:along_y + height, along_z:along_z + depth])
    stacked = jnp.stack(shifted, 0)
    return stacked.reshape(27 * padded.shape[0], planes * height * depth)

def avg_pool(field):
    chans, planes, height, depth = field.shape
    return field.reshape(chans, planes // 2, 2, height // 2, 2, depth // 2, 2).mean(axis=(2, 4, 6))

def unpool(grad):
    chans, planes, height, depth = grad.shape
    spread = jnp.broadcast_to(grad[:, :, None, :, None, :, None], (chans, planes, 2, height, 2, depth, 2))
    return spread.reshape(chans, -1) * 0.125

def pad_all(field):
    return jnp.pad(field, ((0, 0), (1, 1), (1, 1), (1, 1)))

def volume_step(slab, cotan, first_weight, first_bias, second_weight, second_bias):
    filters_one = first_weight.shape[0]
    filters_two = second_weight.shape[0]
    planes, height, depth = (slab.shape[1], slab.shape[2], slab.shape[3])
    half_p, half_y, half_z = (planes // 2, height // 2, depth // 2)
    stacked_first = columns(pad_all(slab), planes, height, depth)
    pre_first = jnp.dot(first_weight, stacked_first, preferred_element_type=jnp.float32) + first_bias[:, None]
    act_first = jnp.where(pre_first > 0, pre_first, leak_slope * pre_first)
    pooled = avg_pool(act_first.reshape(filters_one, planes, height, depth)).astype(jnp.bfloat16)
    stacked_second = columns(pad_all(pooled), half_p, half_y, half_z)
    pre_second = jnp.dot(second_weight, stacked_second, preferred_element_type=jnp.float32) + second_bias[:, None]
    activation = jnp.where(pre_second > 0, pre_second, leak_slope * pre_second).astype(jnp.bfloat16)
    slope_second = jnp.where(pre_second > 0, 1.0, leak_slope)
    grad_pre_second = (cotan.reshape(filters_two, -1).astype(jnp.float32) * slope_second).astype(jnp.bfloat16)
    dims = (((1,), (1,)), ((), ()))
    grad_second_weight = lax.dot_general(grad_pre_second, stacked_second, dims, preferred_element_type=jnp.float32)
    grad_second_bias = lax.optimization_barrier(jnp.sum(grad_pre_second.astype(jnp.float32), axis=1))
    stacked_back = columns(pad_all(grad_pre_second.reshape(filters_two, half_p, half_y, half_z)), half_p, half_y, half_z)
    flipped = second_weight.reshape(filters_two, 27, filters_one)[:, ::-1, :].transpose(2, 1, 0).reshape(filters_one, 27 * filters_two)
    grad_pooled = jnp.dot(flipped, stacked_back, preferred_element_type=jnp.float32)
    slope_first = jnp.where(pre_first > 0, 1.0, leak_slope)
    grad_pre_first = (unpool(grad_pooled.reshape(filters_one, half_p, half_y, half_z)) * slope_first).astype(jnp.bfloat16)
    grad_first_weight = lax.dot_general(grad_pre_first, stacked_first, dims, preferred_element_type=jnp.float32)
    grad_first_bias = lax.optimization_barrier(jnp.sum(grad_pre_first.astype(jnp.float32), axis=1))
    activation = activation.reshape(filters_two, half_p, half_y, half_z)
    return (activation, grad_first_weight, grad_first_bias, grad_second_weight, grad_second_bias)

def reference(volume, first_weight, first_bias, second_weight, second_bias, cotangent):

    def per_volume(pieces):
        return volume_step(pieces[0], pieces[1], first_weight, first_bias, second_weight, second_bias)
    results = lax.map(per_volume, (volume, cotangent))
    count_first = float(volume.shape[0] * NX * SY * SZ)
    scale_first = 1.0 / math.sqrt(count_first)
    scale_second = 1.0 / math.sqrt(count_first / 8.0)
    return (results[0], lax.optimization_barrier(jnp.sum(results[1], axis=0)) * scale_first, lax.optimization_barrier(jnp.sum(results[2], axis=0)) * scale_first, lax.optimization_barrier(jnp.sum(results[3], axis=0)) * scale_second, lax.optimization_barrier(jnp.sum(results[4], axis=0)) * scale_second)
```

```python
import math

import jax
import jax.numpy as jnp
import numpy as np
from jax import lax
from jax.experimental import pallas as pl
from jax.experimental.pallas import tpu as pltpu
from jax.sharding import Mesh, PartitionSpec as P

leak_slope = 0.3
F32, BF16 = jnp.float32, jnp.bfloat16
HALO = 5
NT = (((1,), (1,)), ((), ()))


def split_matrix():
    d = np.zeros((256, 4, 128), np.float32)
    for dz in range(4):
        for k in range(128):
            z = 2 * k - 1 + dz
            if 0 <= z < 256:
                d[z, dz, k] = 1.0
    return d.reshape(256, 512)


def spread_matrix():
    sel = np.zeros((27, 4, 8, 4, 4, 4, 4), np.float32)
    for s in range(8):
        sz, sx, sy = s // 4, s // 2 % 2, s % 2
        for t in range(27):
            tx, ty, tz = t // 9, t // 3 % 3, t % 3
            for c in range(4):
                sel[t, c, s, tx + sx, ty + sy, tz + sz, c] = 1.0
    return sel.reshape(108, 2048)


def compact_matrix():
    m = np.zeros((256, 128), np.float32)
    for g in range(9):
        for j in range(12):
            m[g * 16 + j, g * 12 + j] = 1.0
    return m


def prepare_kernel(w1_ref, w2_ref, sel_ref, w1big_ref, wexp_ref, wt_ref, w2_pad):
    for s in range(8):
        w1big_ref[s * 32 : (s + 1) * 32, :] = jnp.dot(
            w1_ref[...], sel_ref[:, s * 256 : (s + 1) * 256], preferred_element_type=F32
        ).astype(BF16)
    w2_pad[:, 768:1024] = jnp.zeros((64, 256), F32)
    w2_pad[:, 0:864] = w2_ref[...].astype(F32)
    lane = lax.broadcasted_iota(jnp.int32, (64, 128), 1)
    zero = jnp.zeros((64, 128), F32)
    units = []
    for u in range(9):
        start = 96 * u // 128 * 128
        window = w2_pad[:, start : start + 256]
        if 96 * u > start:
            window = pltpu.roll(window, 256 - (96 * u - start), 1)
        units.append(jnp.where(lane < 96, window[:, :128], 0.0))
    for dx in range(3):
        for yin in range(4):
            at = (dx * 4 + yin) * 128
            rows = []
            for y in range(4):
                dy = yin - y + 1
                rows.append(units[dx * 3 + dy] if 0 <= dy <= 2 else zero)
            for pair in range(2):
                block = jnp.concatenate(rows[2 * pair : 2 * pair + 2], axis=0)
                wexp_ref[pair * 128 : (pair + 1) * 128, at : at + 128] = block.astype(BF16)
                col = (2 - dx) * 256 + pair * 128
                wt_ref[yin * 96 : (yin + 1) * 96, col : col + 128] = block.T[:96].astype(BF16)


def main_kernel(
    place_ref, vol_ref, vlo_ref, vhi_ref, cot_ref, clo_ref, chi_ref, split_ref, compact_ref,
    w1_ref, b1_ref, wexp_ref, b2_ref, wt_ref,
    act_ref, grad_ref,
    fine, win, ps, g2s, pre_s,
    *, scale_first, scale_second,
):
    place = place_ref[0]
    last = place_ref[1]
    x0 = 0
    for ref, count in ((vlo_ref, HALO), (vol_ref, 8), (vhi_ref, HALO)):
        rows = ref[...].astype(F32).reshape(4 * count * 8, 256).astype(BF16)
        parts = jnp.dot(rows, split_ref[...], preferred_element_type=F32)
        for c in range(4):
            for x in range(count):
                for dz in range(4):
                    fine[pl.ds((x0 + x) * 128 + dz * 32 + c * 8, 8), :] = parts[
                        (c * count + x) * 8 : (c * count + x + 1) * 8, dz * 128 : (dz + 1) * 128
                    ]
        x0 += count
    for x in range(8 + 2 * HALO):
        win[x, 0:16, :] = jnp.zeros((16, 128), BF16)
        win[x, 144:160, :] = jnp.zeros((16, 128), BF16)
        for y in range(8):
            win[x, (y + 1) * 16 : (y + 2) * 16, :] = fine[pl.ds(x * 128 + y, 16, stride=8), :].astype(BF16)

    def window(q, y):
        return jnp.concatenate([win[2 * q + dx, 32 * y : 32 * y + 64, :] for dx in range(4)], axis=0)

    lane = lax.broadcasted_iota(jnp.int32, (32, 128), 1)
    bias1 = b1_ref[...]
    bias1 = jnp.concatenate([bias1, bias1], axis=1)
    bias2 = b2_ref[...]
    bias2 = jnp.concatenate([bias2, bias2], axis=1)
    ones = jnp.ones((32, 128), BF16)
    for q in range(8):
        for yp in range(2):
            y0 = 2 * yp
            both = jnp.concatenate([window(q, y0), window(q, y0 + 1)], axis=1)
            pre = jnp.dot(w1_ref[...], both, preferred_element_type=F32) + bias1
            if 2 <= q < 6:
                for i in range(2):
                    pre_s[(q - 2) * 4 + y0 + i] = pre[:, i * 128 : (i + 1) * 128].astype(BF16)
            act = jnp.maximum(pre, leak_slope * pre)
            total = act[0:32]
            for s in range(1, 8):
                total = total + act[s * 32 : (s + 1) * 32]
            total = total * 0.125
            if q < 2:
                total = jnp.where(place > 0, total, 0.0)
            if q >= 6:
                total = jnp.where(place < last, total, 0.0)
            for i in range(2):
                pooled = total[:, i * 128 : (i + 1) * 128]
                at = q * 512 + (y0 + i) * 128
                ps[at : at + 32, :] = jnp.where(lane == 0, 0.0, pltpu.roll(pooled, 1, 1)).astype(BF16)
                ps[at + 32 : at + 64, :] = pooled.astype(BF16)
                ps[at + 64 : at + 96, :] = jnp.where(lane == 127, 0.0, pltpu.roll(pooled, 127, 1)).astype(BF16)
                ps[at + 96 : at + 128, :] = ones

    for r0 in range(0, 6, 2):
        both = jnp.concatenate([ps[r * 512 : (r + 3) * 512, :] for r in (r0, r0 + 1)], axis=1)
        pre = jnp.dot(wexp_ref[...], both, preferred_element_type=F32) + bias2
        act = jnp.maximum(pre, leak_slope * pre)
        for i in range(2):
            r = r0 + i
            cot = (clo_ref[...] if r == 0 else chi_ref[...] if r == 5 else cot_ref[r - 1]).astype(F32)
            own = pre[:, i * 128 : (i + 1) * 128]
            g2s[r * 256 : (r + 1) * 256, :] = jnp.where(own > 0, cot, leak_slope * cot).astype(BF16)
            if 1 <= r <= 4:
                act_ref[r - 1] = act[:, i * 128 : (i + 1) * 128].astype(BF16)

    lane96 = lax.broadcasted_iota(jnp.int32, (96, 128), 1)
    grads = jnp.concatenate([g2s[(p + 1) * 256 : (p + 2) * 256, :] for p in range(4)], axis=1)
    folded = []
    b2_grad = None
    for dx in range(3):
        cols = jnp.concatenate([ps[(p + 1 + dx) * 512 : (p + 2 + dx) * 512, :] for p in range(4)], axis=1)
        t = lax.dot_general(cols, grads, NT, preferred_element_type=F32)
        if dx == 0:
            b2_grad = t[96:104, 0:128] + t[96:104, 128:256]
        for dy in range(3):
            sums = []
            for parity in range(2):
                total = None
                for y in (parity, parity + 2):
                    yin = y + dy - 1
                    if 0 <= yin < 4:
                        piece = t[yin * 128 : yin * 128 + 96, (y // 2) * 128 : (y // 2 + 1) * 128]
                        total = piece if total is None else total + piece
                sums.append(total)
            u = jnp.where(lane96 < 64, sums[0], sums[1])
            folded.append(u + pltpu.roll(u, 64, 1))
    folded = jnp.concatenate(folded + [jnp.zeros((160, 128), F32)], axis=0) * scale_second
    lane128 = lax.broadcasted_iota(jnp.int32, (128, 128), 1)
    for j in range(0, 8, 2):
        two = jnp.where(lane128 < 64, folded[j * 128 : (j + 1) * 128], folded[(j + 1) * 128 : (j + 2) * 128]).T
        grad_ref[j] = two[:64]
        if j < 6:
            grad_ref[j + 1] = two[64:]

    ones16 = jnp.ones((16, 512), BF16)
    m1 = None
    for pp in range(2):
        q = jnp.dot(
            wt_ref[...],
            jnp.concatenate([g2s[p * 256 : (p + 3) * 256, :] for p in (2 * pp, 2 * pp + 1)], axis=1),
            preferred_element_type=F32,
        )
        for i in range(2):
            p = 2 * pp + i
            cells = []
            for y in range(4):
                three = q[y * 96 : (y + 1) * 96, i * 128 : (i + 1) * 128] * 0.125
                g = (
                    jnp.where(lane == 127, 0.0, pltpu.roll(three[0:32], 127, 1))
                    + three[32:64]
                    + jnp.where(lane == 0, 0.0, pltpu.roll(three[64:96], 1, 1))
                )
                low = leak_slope * g
                pre = pre_s[p * 4 + y].astype(F32)
                cells.append(
                    jnp.concatenate(
                        [jnp.where(pre[s * 32 : (s + 1) * 32] > 0, g, low) for s in range(8)], axis=0
                    ).astype(BF16)
                )
            cols = jnp.concatenate([window(p + 2, y) for y in range(4)], axis=1)
            cols = jnp.concatenate([cols, ones16], axis=0)
            t = lax.dot_general(cols, jnp.concatenate(cells, axis=1), NT, preferred_element_type=F32)
            m1 = t if m1 is None else m1 + t

    lane16 = lax.broadcasted_iota(jnp.int32, (16, 128), 1)
    half = []
    for g in range(16):
        half.append(m1[g * 16 : (g + 1) * 16, 0:128] + pltpu.roll(m1[g * 16 : (g + 1) * 16, 128:256], 12, 0))
    groups = []
    for tx in range(3):
        for ty in range(3):
            a = half[tx * 4 + ty]
            b = half[tx * 4 + ty + 1]
            c = half[(tx + 1) * 4 + ty]
            d = half[(tx + 1) * 4 + ty + 1]
            v = jnp.where(lane16 < 32, a, jnp.where(lane16 < 64, b, jnp.where(lane16 < 96, c, d)))
            v = v + pltpu.roll(v, 64, 1)
            groups.append(v + pltpu.roll(v, 32, 1))
    first = jnp.concatenate(groups[:8], axis=0).T[:32]
    ninth = jnp.concatenate([groups[8], jnp.zeros((112, 128), F32)], axis=0).T[:32]
    w1_grad = jnp.dot(
        jnp.concatenate([first, ninth], axis=1),
        compact_ref[...],
        precision=lax.Precision.HIGHEST,
        preferred_element_type=F32,
    )
    b1_grad = m1[256:264, 0:128] + m1[256:264, 128:256]
    b1_grad = b1_grad + pltpu.roll(b1_grad, 64, 1)
    b1_grad = b1_grad + pltpu.roll(b1_grad, 32, 1)
    b2_grad = b2_grad + pltpu.roll(b2_grad, 64, 1)
    grad_ref[7, 0:32, :] = w1_grad * scale_first
    grad_ref[7, 32:40, :] = b1_grad * scale_first
    grad_ref[7, 40:48, :] = b2_grad * scale_second
    grad_ref[7, 48:64, :] = jnp.zeros((16, 128), F32)


def unpack_kernel(total_ref, w1_ref, b1_ref, w2_ref, b2_ref):
    for j in range(6):
        w2_ref[:, j * 128 : (j + 1) * 128] = total_ref[j].astype(F32)
    w2_ref[:, 768:864] = total_ref[6].astype(F32)[:, :96]
    rest = total_ref[7].astype(F32)
    w1_ref[...] = rest[0:32, 0:108]
    b1_ref[...] = rest[32:33, 0:32]
    b2_ref[...] = rest[40:41, 0:64]


def exchange(x, axes, count):
    sent = jnp.broadcast_to(x[None], (count,) + x.shape)
    return lax.all_to_all(sent, axes, 0, 0, tiled=True)


def sum_everywhere(packed):
    part = lax.all_to_all(packed, ("x", "c"), 0, 0, tiled=True)
    part = jnp.sum(part.astype(F32), axis=0)
    part = jnp.sum(exchange(part, ("yh", "yl"), 8), axis=0)
    part = jnp.sum(exchange(part, "z", 8), axis=0)
    return exchange(part, ("x", "c"), 8)


def local_step(volume, w1, b1, w2, b2, cotangent, space, count, cells):
    vol, cot = volume[0], cotangent[0]
    forward = [(i, i + 1) for i in range(count - 1)]
    backward = [(i + 1, i) for i in range(count - 1)]
    planes = vol.shape[1]
    edge = lambda plane: cot[:, plane].transpose(1, 0, 2).reshape(256, 128)
    vlo = lax.ppermute(vol[:, planes - HALO :], space, forward)
    vhi = lax.ppermute(vol[:, :HALO], space, backward)
    clo = lax.ppermute(edge(cot.shape[1] - 1), space, forward)
    chi = lax.ppermute(edge(0), space, backward)
    cot = cot.transpose(1, 2, 0, 3).reshape(4, 256, 128)
    w1big, wexp, wt = pl.pallas_call(
        prepare_kernel,
        out_shape=(
            jax.ShapeDtypeStruct((256, 256), BF16),
            jax.ShapeDtypeStruct((256, 1536), BF16),
            jax.ShapeDtypeStruct((384, 768), BF16),
        ),
        scratch_shapes=[pltpu.VMEM((64, 1024), F32)],
        compiler_params=pltpu.CompilerParams(vmem_limit_bytes=16 * 2**20),
        cost_estimate=pl.CostEstimate(flops=20_000_000, bytes_accessed=2_000_000, transcendentals=0),
        name="prepare",
    )(w1, w2, jnp.asarray(spread_matrix(), BF16))
    place = jnp.stack([lax.axis_index(space), jnp.int32(count - 1)]).astype(jnp.int32)
    b1x = jnp.broadcast_to(jnp.tile(b1, 8)[:, None], (256, 128))
    b2x = jnp.broadcast_to(jnp.tile(b2, 4)[:, None], (256, 128))

    def kernel(*refs):
        main_kernel(*refs, scale_first=1.0 / math.sqrt(cells), scale_second=1.0 / math.sqrt(cells / 8.0))

    vmem = pl.BlockSpec(memory_space=pltpu.VMEM)
    act, packed = pl.pallas_call(
        kernel,
        out_shape=(
            jax.ShapeDtypeStruct((4, 256, 128), BF16),
            jax.ShapeDtypeStruct((8, 64, 128), F32),
        ),
        in_specs=[pl.BlockSpec(memory_space=pltpu.SMEM)] + [vmem] * 13,
        out_specs=(vmem, vmem),
        scratch_shapes=[
            pltpu.VMEM((18 * 128, 128), F32),
            pltpu.VMEM((18, 160, 128), BF16),
            pltpu.VMEM((8 * 512, 128), BF16),
            pltpu.VMEM((6 * 256, 128), BF16),
            pltpu.VMEM((16, 256, 128), BF16),
        ],
        compiler_params=pltpu.CompilerParams(vmem_limit_bytes=48 * 2**20),
        cost_estimate=pl.CostEstimate(flops=3_000_000_000, bytes_accessed=4_000_000, transcendentals=0),
        name="layers",
    )(
        place, vol, vlo, vhi, cot, clo, chi,
        jnp.asarray(split_matrix(), BF16), jnp.asarray(compact_matrix(), F32),
        w1big, b1x, wexp, b2x, wt,
    )
    act = act.reshape(4, 4, 64, 128).transpose(2, 0, 1, 3)[None]
    return act, packed


def solution(mesh):
    dp, space = mesh.shape["dp"], mesh.shape["space"]
    split = Mesh(mesh.devices.reshape(8, 2, 4, 4, 2), ("z", "yh", "x", "yl", "c"))
    along = ("x", "yl", "c")

    def on_device(volume, w1, b1, w2, b2, cotangent):
        cells = float(math.prod(volume.shape[2:]) * dp * space)
        act, packed = local_step(volume, w1, b1, w2, b2, cotangent, along, space, cells)
        total = sum_everywhere(packed)
        gw1, gb1, gw2, gb2 = pl.pallas_call(
            unpack_kernel,
            out_shape=(
                jax.ShapeDtypeStruct((32, 108), F32),
                jax.ShapeDtypeStruct((1, 32), F32),
                jax.ShapeDtypeStruct((64, 864), F32),
                jax.ShapeDtypeStruct((1, 64), F32),
            ),
            name="unpack",
        )(total)
        return act, gw1, gb1[0], gw2, gb2[0]

    shared = P(("z", "yh"), None, along, None, None)
    return jax.shard_map(
        on_device,
        mesh=split,
        in_specs=(shared, P(), P(), P(), P(), shared),
        out_specs=(shared, P(), P(), P(), P()),
        check_vma=False,
    )
```

```python
import math

import jax
import jax.numpy as jnp
import numpy as np
from jax import lax
from jax.experimental import pallas as pl
from jax.experimental.pallas import tpu as pltpu
from jax.sharding import Mesh, PartitionSpec as P

leak_slope = 0.3
F32, BF16 = jnp.float32, jnp.bfloat16
HALO = 5
NT = (((1,), (1,)), ((), ()))


def split_matrix():
    d = np.zeros((256, 4, 128), np.float32)
    for dz in range(4):
        for k in range(128):
            z = 2 * k - 1 + dz
            if 0 <= z < 256:
                d[z, dz, k] = 1.0
    return d.reshape(256, 512)


def spread_matrix():
    sel = np.zeros((27, 4, 8, 4, 4, 4, 4), np.float32)
    for s in range(8):
        sz, sx, sy = s // 4, s // 2 % 2, s % 2
        for t in range(27):
            tx, ty, tz = t // 9, t // 3 % 3, t % 3
            for c in range(4):
                sel[t, c, s, tx + sx, ty + sy, tz + sz, c] = 1.0
    return sel.reshape(108, 2048)


def compact_matrix():
    m = np.zeros((256, 128), np.float32)
    for g in range(9):
        for j in range(12):
            m[g * 16 + j, g * 12 + j] = 1.0
    return m


def prepare_kernel(w1_ref, w2_ref, sel_ref, w1big_ref, wexp_ref, wt_ref, w2_pad):
    for s in range(8):
        w1big_ref[s * 32 : (s + 1) * 32, :] = jnp.dot(
            w1_ref[...], sel_ref[:, s * 256 : (s + 1) * 256], preferred_element_type=F32
        ).astype(BF16)
    w2_pad[:, 768:1024] = jnp.zeros((64, 256), F32)
    w2_pad[:, 0:864] = w2_ref[...].astype(F32)
    lane = lax.broadcasted_iota(jnp.int32, (64, 128), 1)
    zero = jnp.zeros((64, 128), F32)
    units = []
    for u in range(9):
        start = 96 * u // 128 * 128
        window = w2_pad[:, start : start + 256]
        if 96 * u > start:
            window = pltpu.roll(window, 256 - (96 * u - start), 1)
        units.append(jnp.where(lane < 96, window[:, :128], 0.0))
    for dx in range(3):
        for yin in range(4):
            at = (dx * 4 + yin) * 128
            rows = []
            for y in range(4):
                dy = yin - y + 1
                rows.append(units[dx * 3 + dy] if 0 <= dy <= 2 else zero)
            for pair in range(2):
                block = jnp.concatenate(rows[2 * pair : 2 * pair + 2], axis=0)
                wexp_ref[pair * 128 : (pair + 1) * 128, at : at + 128] = block.astype(BF16)
                col = (2 - dx) * 256 + pair * 128
                wt_ref[yin * 96 : (yin + 1) * 96, col : col + 128] = block.T[:96].astype(BF16)


def main_kernel(
    place_ref, vol_ref, low_ref, high_ref, cot_ref, split_ref, compact_ref,
    w1_ref, b1_ref, wexp_ref, b2_ref, wt_ref,
    act_ref, grad_ref,
    fine, win, ps, g2s, pre_s,
    *, scale_first, scale_second,
):
    place = place_ref[0]
    last = place_ref[1]
    x0 = 0
    for ref, count in ((low_ref, HALO), (vol_ref, 8), (high_ref, HALO)):
        if ref is vol_ref:
            rows = ref[...].astype(F32).reshape(4 * count * 8, 256).astype(BF16)
        else:
            rows = ref[0 : 4 * count * 8, :]
        parts = jnp.dot(rows, split_ref[...], preferred_element_type=F32)
        for c in range(4):
            for x in range(count):
                for dz in range(4):
                    fine[pl.ds((x0 + x) * 128 + dz * 32 + c * 8, 8), :] = parts[
                        (c * count + x) * 8 : (c * count + x + 1) * 8, dz * 128 : (dz + 1) * 128
                    ]
        x0 += count
    for x in range(8 + 2 * HALO):
        win[x, 0:16, :] = jnp.zeros((16, 128), BF16)
        win[x, 144:160, :] = jnp.zeros((16, 128), BF16)
        for y in range(8):
            win[x, (y + 1) * 16 : (y + 2) * 16, :] = fine[pl.ds(x * 128 + y, 16, stride=8), :].astype(BF16)

    def window(q, y):
        return jnp.concatenate([win[2 * q + dx, 32 * y : 32 * y + 64, :] for dx in range(4)], axis=0)

    lane = lax.broadcasted_iota(jnp.int32, (32, 128), 1)
    bias1 = b1_ref[...]
    bias1 = jnp.concatenate([bias1, bias1], axis=1)
    bias2 = b2_ref[...]
    bias2 = jnp.concatenate([bias2, bias2], axis=1)
    ones = jnp.ones((32, 128), BF16)
    for q in range(8):
        for yp in range(2):
            y0 = 2 * yp
            both = jnp.concatenate([window(q, y0), window(q, y0 + 1)], axis=1)
            pre = jnp.dot(w1_ref[...], both, preferred_element_type=F32) + bias1
            if 2 <= q < 6:
                for i in range(2):
                    pre_s[(q - 2) * 4 + y0 + i] = pre[:, i * 128 : (i + 1) * 128].astype(BF16)
            act = jnp.maximum(pre, leak_slope * pre)
            total = act[0:32]
            for s in range(1, 8):
                total = total + act[s * 32 : (s + 1) * 32]
            total = total * 0.125
            if q < 2:
                total = jnp.where(place > 0, total, 0.0)
            if q >= 6:
                total = jnp.where(place < last, total, 0.0)
            for i in range(2):
                pooled = total[:, i * 128 : (i + 1) * 128]
                at = q * 512 + (y0 + i) * 128
                ps[at : at + 32, :] = jnp.where(lane == 0, 0.0, pltpu.roll(pooled, 1, 1)).astype(BF16)
                ps[at + 32 : at + 64, :] = pooled.astype(BF16)
                ps[at + 64 : at + 96, :] = jnp.where(lane == 127, 0.0, pltpu.roll(pooled, 127, 1)).astype(BF16)
                ps[at + 96 : at + 128, :] = ones

    for r0 in range(0, 6, 2):
        both = jnp.concatenate([ps[r * 512 : (r + 3) * 512, :] for r in (r0, r0 + 1)], axis=1)
        pre = jnp.dot(wexp_ref[...], both, preferred_element_type=F32) + bias2
        act = jnp.maximum(pre, leak_slope * pre)
        for i in range(2):
            r = r0 + i
            if 1 <= r <= 4:
                cot = cot_ref[r - 1].astype(F32)
            else:
                sent = (low_ref if r == 0 else high_ref)[160:288, :].astype(F32)
                cot = jnp.concatenate(
                    [sent[0:64, 0:128], sent[64:128, 0:128], sent[0:64, 128:256], sent[64:128, 128:256]], axis=0
                )
            own = pre[:, i * 128 : (i + 1) * 128]
            g2s[r * 256 : (r + 1) * 256, :] = jnp.where(own > 0, cot, leak_slope * cot).astype(BF16)
            if 1 <= r <= 4:
                act_ref[r - 1] = act[:, i * 128 : (i + 1) * 128].astype(BF16)

    lane96 = lax.broadcasted_iota(jnp.int32, (96, 128), 1)
    grads = jnp.concatenate([g2s[(p + 1) * 256 : (p + 2) * 256, :] for p in range(4)], axis=1)
    folded = []
    b2_grad = None
    for dx in range(3):
        cols = jnp.concatenate([ps[(p + 1 + dx) * 512 : (p + 2 + dx) * 512, :] for p in range(4)], axis=1)
        t = lax.dot_general(cols, grads, NT, preferred_element_type=F32)
        if dx == 0:
            b2_grad = t[96:104, 0:128] + t[96:104, 128:256]
        for dy in range(3):
            sums = []
            for parity in range(2):
                total = None
                for y in (parity, parity + 2):
                    yin = y + dy - 1
                    if 0 <= yin < 4:
                        piece = t[yin * 128 : yin * 128 + 96, (y // 2) * 128 : (y // 2 + 1) * 128]
                        total = piece if total is None else total + piece
                sums.append(total)
            u = jnp.where(lane96 < 64, sums[0], sums[1])
            folded.append(u + pltpu.roll(u, 64, 1))
    folded = jnp.concatenate(folded + [jnp.zeros((160, 128), F32)], axis=0) * scale_second
    lane128 = lax.broadcasted_iota(jnp.int32, (128, 128), 1)
    for j in range(0, 8, 2):
        two = jnp.where(lane128 < 64, folded[j * 128 : (j + 1) * 128], folded[(j + 1) * 128 : (j + 2) * 128]).T
        grad_ref[j] = two[:64].astype(BF16)
        if j < 6:
            grad_ref[j + 1] = two[64:].astype(BF16)

    ones16 = jnp.ones((16, 512), BF16)
    m1 = None
    for pp in range(2):
        q = jnp.dot(
            wt_ref[...],
            jnp.concatenate([g2s[p * 256 : (p + 3) * 256, :] for p in (2 * pp, 2 * pp + 1)], axis=1),
            preferred_element_type=F32,
        )
        for i in range(2):
            p = 2 * pp + i
            cells = []
            for y in range(4):
                three = q[y * 96 : (y + 1) * 96, i * 128 : (i + 1) * 128] * 0.125
                g = (
                    jnp.where(lane == 127, 0.0, pltpu.roll(three[0:32], 127, 1))
                    + three[32:64]
                    + jnp.where(lane == 0, 0.0, pltpu.roll(three[64:96], 1, 1))
                )
                low = leak_slope * g
                pre = pre_s[p * 4 + y].astype(F32)
                cells.append(
                    jnp.concatenate(
                        [jnp.where(pre[s * 32 : (s + 1) * 32] > 0, g, low) for s in range(8)], axis=0
                    ).astype(BF16)
                )
            cols = jnp.concatenate([window(p + 2, y) for y in range(4)], axis=1)
            cols = jnp.concatenate([cols, ones16], axis=0)
            t = lax.dot_general(cols, jnp.concatenate(cells, axis=1), NT, preferred_element_type=F32)
            m1 = t if m1 is None else m1 + t

    lane16 = lax.broadcasted_iota(jnp.int32, (16, 128), 1)
    half = []
    for g in range(16):
        half.append(m1[g * 16 : (g + 1) * 16, 0:128] + pltpu.roll(m1[g * 16 : (g + 1) * 16, 128:256], 12, 0))
    groups = []
    for tx in range(3):
        for ty in range(3):
            a = half[tx * 4 + ty]
            b = half[tx * 4 + ty + 1]
            c = half[(tx + 1) * 4 + ty]
            d = half[(tx + 1) * 4 + ty + 1]
            v = jnp.where(lane16 < 32, a, jnp.where(lane16 < 64, b, jnp.where(lane16 < 96, c, d)))
            v = v + pltpu.roll(v, 64, 1)
            groups.append(v + pltpu.roll(v, 32, 1))
    first = jnp.concatenate(groups[:8], axis=0).T[:32]
    ninth = jnp.concatenate([groups[8], jnp.zeros((112, 128), F32)], axis=0).T[:32]
    w1_grad = jnp.dot(
        jnp.concatenate([first, ninth], axis=1),
        compact_ref[...],
        precision=lax.Precision.HIGHEST,
        preferred_element_type=F32,
    )
    b1_grad = m1[256:264, 0:128] + m1[256:264, 128:256]
    b1_grad = b1_grad + pltpu.roll(b1_grad, 64, 1)
    b1_grad = b1_grad + pltpu.roll(b1_grad, 32, 1)
    b2_grad = b2_grad + pltpu.roll(b2_grad, 64, 1)
    biases = jnp.concatenate([b1_grad * scale_first, b2_grad * scale_second], axis=0)
    grad_ref[7, 0:32, :] = (w1_grad * scale_first).astype(BF16)
    grad_ref[7, 32:48, :] = biases.astype(BF16)
    grad_ref[7, 48:64, :] = jnp.zeros((16, 128), BF16)


def unpack_kernel(total_ref, w1_ref, b1_ref, w2_ref, b2_ref):
    for j in range(6):
        w2_ref[:, j * 128 : (j + 1) * 128] = total_ref[j].astype(F32)
    w2_ref[:, 768:864] = total_ref[6].astype(F32)[:, :96]
    rest = total_ref[7].astype(F32)
    w1_ref[...] = rest[0:32, 0:108]
    b1_ref[...] = rest[32:33, 0:32]
    b2_ref[...] = rest[40:41, 0:64]


def exchange(x, axes, count):
    sent = jnp.broadcast_to(x.astype(BF16)[None], (count,) + x.shape)
    return lax.all_to_all(sent, axes, 0, 0, tiled=True)


def add(parts):
    return jnp.sum(parts.astype(F32), axis=0)


def sum_everywhere(packed):
    part = add(lax.all_to_all(packed, ("x", "c"), 0, 0, tiled=True))
    part = add(exchange(part, ("yh", "yl"), 8))
    part = add(exchange(part, "z", 8))
    return exchange(part, ("x", "c"), 8)


def local_step(volume, w1, b1, w2, b2, cotangent, space, count, cells):
    vol, cot = volume[0], cotangent[0]
    forward = [(i, i + 1) for i in range(count - 1)]
    backward = [(i + 1, i) for i in range(count - 1)]
    planes = vol.shape[1]

    def edge(first, plane):
        planes_sent = vol[:, first : first + HALO].reshape(160, 256)
        rows = cot[:, plane].reshape(64, 2, 2, 128).transpose(2, 0, 1, 3).reshape(128, 256)
        return jnp.concatenate([planes_sent, rows], axis=0)

    low = lax.ppermute(edge(planes - HALO, cot.shape[1] - 1), space, forward)
    high = lax.ppermute(edge(0, 0), space, backward)
    cot = cot.transpose(1, 2, 0, 3).reshape(4, 256, 128)
    w1big, wexp, wt = pl.pallas_call(
        prepare_kernel,
        out_shape=(
            jax.ShapeDtypeStruct((256, 256), BF16),
            jax.ShapeDtypeStruct((256, 1536), BF16),
            jax.ShapeDtypeStruct((384, 768), BF16),
        ),
        scratch_shapes=[pltpu.VMEM((64, 1024), F32)],
        compiler_params=pltpu.CompilerParams(vmem_limit_bytes=16 * 2**20),
        cost_estimate=pl.CostEstimate(flops=20_000_000, bytes_accessed=2_000_000, transcendentals=0),
        name="prepare",
    )(w1, w2, jnp.asarray(spread_matrix(), BF16))
    place = jnp.stack([lax.axis_index(space), jnp.int32(count - 1)]).astype(jnp.int32)
    b1x = jnp.broadcast_to(jnp.tile(b1, 8)[:, None], (256, 128))
    b2x = jnp.broadcast_to(jnp.tile(b2, 4)[:, None], (256, 128))

    def kernel(*refs):
        main_kernel(*refs, scale_first=1.0 / math.sqrt(cells), scale_second=1.0 / math.sqrt(cells / 8.0))

    vmem = pl.BlockSpec(memory_space=pltpu.VMEM)
    act, packed = pl.pallas_call(
        kernel,
        out_shape=(
            jax.ShapeDtypeStruct((4, 256, 128), BF16),
            jax.ShapeDtypeStruct((8, 64, 128), BF16),
        ),
        in_specs=[pl.BlockSpec(memory_space=pltpu.SMEM)] + [vmem] * 11,
        out_specs=(vmem, vmem),
        scratch_shapes=[
            pltpu.VMEM((18 * 128, 128), F32),
            pltpu.VMEM((18, 160, 128), BF16),
            pltpu.VMEM((8 * 512, 128), BF16),
            pltpu.VMEM((6 * 256, 128), BF16),
            pltpu.VMEM((16, 256, 128), BF16),
        ],
        compiler_params=pltpu.CompilerParams(vmem_limit_bytes=48 * 2**20),
        cost_estimate=pl.CostEstimate(flops=3_000_000_000, bytes_accessed=4_000_000, transcendentals=0),
        name="layers",
    )(
        place, vol, low, high, cot,
        jnp.asarray(split_matrix(), BF16), jnp.asarray(compact_matrix(), F32),
        w1big, b1x, wexp, b2x, wt,
    )
    act = act.reshape(4, 4, 64, 128).transpose(2, 0, 1, 3)[None]
    return act, packed


def solution(mesh):
    dp, space = mesh.shape["dp"], mesh.shape["space"]
    split = Mesh(mesh.devices.reshape(8, 2, 4, 4, 2), ("z", "yh", "x", "yl", "c"))
    along = ("x", "yl", "c")

    def on_device(volume, w1, b1, w2, b2, cotangent):
        cells = float(math.prod(volume.shape[2:]) * dp * space)
        act, packed = local_step(volume, w1, b1, w2, b2, cotangent, along, space, cells)
        total = sum_everywhere(packed)
        gw1, gb1, gw2, gb2 = pl.pallas_call(
            unpack_kernel,
            out_shape=(
                jax.ShapeDtypeStruct((32, 108), F32),
                jax.ShapeDtypeStruct((1, 32), F32),
                jax.ShapeDtypeStruct((64, 864), F32),
                jax.ShapeDtypeStruct((1, 64), F32),
            ),
            name="unpack",
        )(total)
        return act, gw1, gb1[0], gw2, gb2[0]

    shared = P(("z", "yh"), None, along, None, None)
    return jax.shard_map(
        on_device,
        mesh=split,
        in_specs=(shared, P(), P(), P(), P(), shared),
        out_specs=(shared, P(), P(), P(), P()),
        check_vma=False,
    )
```

```python
import math

import jax
import jax.numpy as jnp
import numpy as np
from jax import lax
from jax.experimental import pallas as pl
from jax.experimental.pallas import tpu as pltpu
from jax.sharding import Mesh, PartitionSpec as P

leak_slope = 0.3
F32, BF16 = jnp.float32, jnp.bfloat16
HALO = 5
NT = (((1,), (1,)), ((), ()))


def edges_kernel(space, vol_ref, cot_ref, pair_ref, other_ref, cot_s, sems):
    second = lax.axis_index(space) % 2
    copies = []
    for side, ref, high in ((0, other_ref, second), (1, pair_ref, 1 - second)):
        copies.append(pltpu.make_async_copy(cot_ref.at[:, high * 3], cot_s.at[side], sems.at[side, 4]))
        for c in range(4):
            source = vol_ref.at[c, pl.ds(high * (8 - HALO), HALO)]
            copies.append(pltpu.make_async_copy(source, ref.at[pl.ds(c * HALO, HALO)], sems.at[side, c]))
    for copy in copies:
        copy.start()
    for copy in copies:
        copy.wait()
    for side, ref in ((0, other_ref), (1, pair_ref)):
        rows = cot_s[side].astype(F32).reshape(256, 128)
        rows = jnp.concatenate([rows[:128], rows[128:]], axis=1)
        ref[4 * HALO : 4 * HALO + 16] = rows.astype(BF16).reshape(16, 8, 256)


def add_kernel(parts_ref, out_ref):
    total = jnp.sum(parts_ref[...].astype(F32), axis=0).astype(BF16)
    for i in range(out_ref.shape[0]):
        out_ref[i] = total


def in_hbm(x):
    return pltpu.with_memory_space_constraint(x, pltpu.HBM)


def cell_shift(s):
    return (s // 2 % 2) * 64 + (s % 2) * 16 + (s // 4) * 4


def split_phases(rows, split, count, fine, win):
    parts = jnp.dot(rows, split, preferred_element_type=F32)
    for c in range(4):
        for x in range(count):
            for dz in range(4):
                fine[pl.ds(x * 128 + dz * 32 + c * 8, 8), :] = parts[
                    (c * count + x) * 8 : (c * count + x + 1) * 8, dz * 128 : (dz + 1) * 128
                ]
    for x in range(count):
        win[x, 0:16, :] = jnp.zeros((16, 128), BF16)
        win[x, 144:160, :] = jnp.zeros((16, 128), BF16)
        for y in range(8):
            win[x, (y + 1) * 16 : (y + 2) * 16, :] = fine[pl.ds(x * 128 + y, 16, stride=8), :].astype(BF16)


def window(planes, y):
    return jnp.concatenate([ref[x, 32 * y : 32 * y + 64, :] for ref, x in planes], axis=0)


def first_layer(planes, w1, bias, keep_pre, keep_pooled, mask):
    lane = lax.broadcasted_iota(jnp.int32, (32, 128), 1)
    for y0 in (0, 2):
        both = jnp.concatenate([window(planes, y0), window(planes, y0 + 1)], axis=1)
        pre = jnp.dot(w1, both, preferred_element_type=F32) + bias
        if keep_pre is not None:
            for i in range(2):
                keep_pre[y0 + i] = pre[:, i * 128 : (i + 1) * 128].astype(BF16)
        act = jnp.maximum(pre, leak_slope * pre)
        total = act[0:32]
        for s in range(1, 8):
            total = total + act[s * 32 : (s + 1) * 32]
        total = mask(total * 0.125)
        for i in range(2):
            pooled = total[:, i * 128 : (i + 1) * 128]
            at = (y0 + i) * 128
            keep_pooled[at : at + 32, :] = jnp.where(lane == 0, 0.0, pltpu.roll(pooled, 1, 1)).astype(BF16)
            keep_pooled[at + 32 : at + 64, :] = pooled.astype(BF16)
            keep_pooled[at + 64 : at + 96, :] = jnp.where(lane == 127, 0.0, pltpu.roll(pooled, 127, 1)).astype(BF16)
            keep_pooled[at + 96 : at + 128, :] = jnp.ones((32, 128), BF16)


def own_kernel(
    vol_hbm, cot_hbm, w1_hbm, w2_hbm, b1_hbm, b2_hbm,
    w1big_ref, wexp_ref, wt_ref, b1_ref, b2_ref, split_ref, compact_ref, cot_out, win, pre_out, pooled_out,
    vol_ref, cot_ref, w1_ref, w2_ref, b1_row, b2_row, rows8, fine, cot_s, w2_pad, sems,
):
    sources = (vol_hbm, w1_hbm, b1_hbm, b2_hbm, w2_hbm, cot_hbm)
    targets = (vol_ref, w1_ref, b1_row, b2_row, w2_ref, cot_ref)
    copies = [pltpu.make_async_copy(x, y, sems.at[i]) for i, (x, y) in enumerate(zip(sources, targets))]
    for copy in copies:
        copy.start()
    row = lax.broadcasted_iota(jnp.int32, (108, 256), 0)
    column = lax.broadcasted_iota(jnp.int32, (108, 256), 1)
    base = row // 36 * 64 + row // 12 % 3 * 16 + row % 12
    spread = jnp.where(column == base, 1.0, 0.0).astype(BF16)
    z = lax.broadcasted_iota(jnp.int32, (256, 128), 0)
    k = lax.broadcasted_iota(jnp.int32, (256, 128), 1)
    for dz in range(4):
        split_ref[:, dz * 128 : (dz + 1) * 128] = jnp.where(z == 2 * k - 1 + dz, 1.0, 0.0).astype(BF16)
    base = k // 36 * 64 + k // 12 % 3 * 16 + k % 12
    compact_ref[...] = jnp.where((z == base) & (k < 108), 1.0, 0.0)
    rows8[...] = jnp.zeros((16, 128), F32)
    w2_pad[...] = jnp.zeros((64, 1024), F32)
    for copy in copies[:4]:
        copy.wait()

    wide = jnp.dot(w1_ref[...], spread, preferred_element_type=F32)
    for s in range(8):
        shift = cell_shift(s)
        moved = pltpu.roll(wide, shift, 1) if shift else wide
        w1big_ref[s * 32 : (s + 1) * 32, :] = moved.astype(BF16)
    rows8[0:1, 0:32] = b1_row[...]
    rows8[8:9, 0:64] = b2_row[...]
    b1 = jnp.broadcast_to(rows8[0:1, :], (128, 128)).T[:32]
    b1_ref[...] = jnp.concatenate([b1] * 8, axis=0)
    b2 = jnp.broadcast_to(rows8[8:9, :], (128, 128)).T[:64]
    b2_ref[...] = jnp.concatenate([b2] * 4, axis=0)

    rows = vol_ref[...].astype(F32).reshape(256, 256).astype(BF16)
    split_phases(rows, split_ref[...], 8, fine, win)
    bias = b1_ref[...]
    bias = jnp.concatenate([bias, bias], axis=1)
    for i in range(2):
        planes = [(win, 1 + 2 * i + dx) for dx in range(4)]
        first_layer(planes, w1big_ref[...], bias, pre_out.at[i], pooled_out.at[i], lambda v: v)

    copies[4].wait()
    w2_pad[:, 0:864] = w2_ref[...].astype(F32)
    lane = lax.broadcasted_iota(jnp.int32, (64, 128), 1)
    zero = jnp.zeros((64, 128), F32)
    units = []
    for u in range(9):
        start = 96 * u // 128 * 128
        part = w2_pad[:, start : start + 256]
        if 96 * u > start:
            part = pltpu.roll(part, 256 - (96 * u - start), 1)
        units.append(jnp.where(lane < 96, part[:, :128], 0.0))
    for dx in range(3):
        for yin in range(4):
            at = (dx * 4 + yin) * 128
            rows = []
            for y in range(4):
                dy = yin - y + 1
                rows.append(units[dx * 3 + dy] if 0 <= dy <= 2 else zero)
            for pair in range(2):
                block = jnp.concatenate(rows[2 * pair : 2 * pair + 2], axis=0)
                wexp_ref[pair * 128 : (pair + 1) * 128, at : at + 128] = block.astype(BF16)
                col = (2 - dx) * 256 + pair * 128
                wt_ref[yin * 96 : (yin + 1) * 96, col : col + 128] = block.T[:96].astype(BF16)

    copies[5].wait()
    cot_s[0:1024, :] = cot_ref[...].astype(F32).reshape(1024, 128)
    for p in range(4):
        for y in range(4):
            cot_out[p, y * 64 : (y + 1) * 64, :] = cot_s[pl.ds(p * 4 + y, 64, stride=16), :].astype(BF16)


def layers_kernel(
    other_ref, pair_ref,
    w1_ref, wexp_ref, wt_ref, b1_ref, b2_ref, split_ref, compact_ref, cot_ref, win, pre_own, pooled_own,
    act_ref, grad_ref,
    halo, fine, win_low, win_high, cot_s, ps, pre_s, g2s, act_s, act_out, sem,
    *, space, last, scale_first, scale_second,
):
    place = lax.axis_index(space)
    second = place % 2

    @pl.when(second == 0)
    def _():
        halo[0] = other_ref[...]
        halo[1] = pair_ref[...]

    @pl.when(second != 0)
    def _():
        halo[0] = pair_ref[...]
        halo[1] = other_ref[...]

    for side, target in ((0, win_low), (1, win_high)):
        rows = halo[side, 0 : 4 * HALO].astype(F32).reshape(160, 256).astype(BF16)
        split_phases(rows, split_ref[...], HALO, fine.at[side], target)

    def plane(x):
        if x < HALO:
            return win_low, x
        if x < HALO + 8:
            return win, x - HALO
        return win_high, x - HALO - 8

    bias1 = b1_ref[...]
    bias1 = jnp.concatenate([bias1, bias1], axis=1)
    bias2 = b2_ref[...]
    bias2 = jnp.concatenate([bias2, bias2], axis=1)
    for q in (0, 1, 2, 5, 6, 7):
        keep = pre_s.at[0] if q == 2 else pre_s.at[1] if q == 5 else None
        if q < 2:
            mask = lambda v: jnp.where(place > 0, v, 0.0)
        elif q > 5:
            mask = lambda v: jnp.where(place < last, v, 0.0)
        else:
            mask = lambda v: v
        first_layer([plane(2 * q + dx) for dx in range(4)], w1_ref[...], bias1, keep, ps.at[q], mask)

    def pooled(q):
        return pooled_own[q - 3] if q in (3, 4) else ps[q]

    def three(r):
        return jnp.concatenate([pooled(r), pooled(r + 1), pooled(r + 2)], axis=0)

    both = jnp.concatenate([three(r) for r in range(6)], axis=1)
    pre = jnp.dot(wexp_ref[...], both, preferred_element_type=F32) + jnp.concatenate([bias2] * 3, axis=1)
    act = jnp.maximum(pre, leak_slope * pre)
    for r in range(6):
        if 1 <= r <= 4:
            cot = cot_ref[r - 1].astype(F32)
            for y in range(4):
                act_s[pl.ds((r - 1) * 4 + y, 64, stride=16), :] = act[
                    y * 64 : (y + 1) * 64, r * 128 : (r + 1) * 128
                ]
        else:
            sent = halo[r // 5, 4 * HALO : 4 * HALO + 16].astype(F32).reshape(128, 256)
            cot_s[0:128, :] = sent[:, 0:128]
            cot_s[128:256, :] = sent[:, 128:256]
            cot = jnp.concatenate([cot_s[pl.ds(y, 64, stride=4), :] for y in range(4)], axis=0)
        own = pre[:, r * 128 : (r + 1) * 128]
        g2s[r * 256 : (r + 1) * 256, :] = jnp.where(own > 0, cot, leak_slope * cot).astype(BF16)
    act_out[...] = act_s[0:1024, :].reshape(64, 16, 128).astype(BF16)
    copy = pltpu.make_async_copy(act_out, act_ref, sem)
    copy.start()

    lane = lax.broadcasted_iota(jnp.int32, (32, 128), 1)
    ones = jnp.ones((8, 512), BF16)
    all_cells, all_cols = [], []
    q = jnp.dot(
        wt_ref[...],
        jnp.concatenate([g2s[p * 256 : (p + 3) * 256, :] for p in range(4)], axis=1),
        preferred_element_type=F32,
    )
    for p in range(4):
        pre_p = pre_own.at[p - 1] if p in (1, 2) else pre_s.at[p // 3]
        cells = []
        for y in range(4):
            taps = q[y * 96 : (y + 1) * 96, p * 128 : (p + 1) * 128] * 0.125
            g = (
                jnp.where(lane == 127, 0.0, pltpu.roll(taps[0:32], 127, 1))
                + taps[32:64]
                + jnp.where(lane == 0, 0.0, pltpu.roll(taps[64:96], 1, 1))
            )
            low = leak_slope * g
            pre = pre_p[y].astype(F32)
            cells.append(
                jnp.concatenate(
                    [jnp.where(pre[s * 32 : (s + 1) * 32] > 0, g, low) for s in range(8)], axis=0
                ).astype(BF16)
            )
        planes = [plane(2 * (p + 2) + dx) for dx in range(4)]
        cols = jnp.concatenate([window(planes, y) for y in range(4)], axis=1)
        cols = jnp.concatenate([cols, ones], axis=0)
        all_cells.append(jnp.concatenate(cells, axis=1))
        all_cols.append(cols)
    m1 = lax.dot_general(
        jnp.concatenate(all_cells, axis=1), jnp.concatenate(all_cols, axis=1), NT, preferred_element_type=F32
    )

    lane96 = lax.broadcasted_iota(jnp.int32, (96, 128), 1)
    grads = jnp.concatenate([g2s[(p + 1) * 256 : (p + 2) * 256, :] for p in range(4)], axis=1)
    folded = []
    b2_grad = None
    cols = jnp.concatenate([jnp.concatenate([pooled(p + 1 + dx) for p in range(4)], axis=1) for dx in range(3)], axis=0)
    tt = lax.dot_general(cols, grads, NT, preferred_element_type=F32)
    for dx in range(3):
        t = tt[dx * 512 : (dx + 1) * 512]
        if dx == 0:
            b2_grad = t[96:104, 0:128] + t[96:104, 128:256]
        for dy in range(3):
            sums = []
            for parity in range(2):
                total = None
                for y in (parity, parity + 2):
                    yin = y + dy - 1
                    if 0 <= yin < 4:
                        piece = t[yin * 128 : yin * 128 + 96, (y // 2) * 128 : (y // 2 + 1) * 128]
                        total = piece if total is None else total + piece
                sums.append(total)
            u = jnp.where(lane96 < 64, sums[0], sums[1])
            folded.append(u + pltpu.roll(u, 64, 1))
    folded = jnp.concatenate(folded + [jnp.zeros((160, 128), F32)], axis=0) * scale_second
    lane128 = lax.broadcasted_iota(jnp.int32, (128, 128), 1)
    for j in range(0, 8, 2):
        two = jnp.where(lane128 < 64, folded[j * 128 : (j + 1) * 128], folded[(j + 1) * 128 : (j + 2) * 128]).T
        grad_ref[j] = two[:64].astype(BF16)
        if j < 6:
            grad_ref[j + 1] = two[64:].astype(BF16)

    total = m1[0:32, 0:256]
    for s in range(1, 8):
        total = total + pltpu.roll(m1[s * 32 : (s + 1) * 32, 0:256], 256 - cell_shift(s), 1)
    w1_grad = jnp.dot(total, compact_ref[...], precision=lax.Precision.HIGHEST, preferred_element_type=F32)
    sums = m1[0:32, 256:257]
    for s in range(1, 8):
        sums = sums + m1[s * 32 : (s + 1) * 32, 256:257]
    b1_grad = jnp.concatenate([jnp.broadcast_to(sums, (32, 128)), jnp.zeros((96, 128), F32)], axis=0).T[:8]
    b2_grad = b2_grad + pltpu.roll(b2_grad, 64, 1)
    biases = jnp.concatenate([b1_grad * scale_first, b2_grad * scale_second], axis=0)
    grad_ref[7, 0:32, :] = (w1_grad * scale_first).astype(BF16)
    grad_ref[7, 32:48, :] = biases.astype(BF16)
    grad_ref[7, 48:64, :] = jnp.zeros((16, 128), BF16)
    copy.wait()


def unpack_kernel(total_ref, w1_ref, b1_ref, w2_ref, b2_ref, w1_s, b1_s, w2_s, b2_s, sems):
    rest = total_ref[7].astype(F32)
    w1_s[...] = rest[0:32, 0:108]
    b1_s[...] = rest[32:33, 0:32]
    b2_s[...] = rest[40:41, 0:64]
    copies = []

    def send(source, target):
        copies.append(pltpu.make_async_copy(source, target, sems.at[len(copies)]))
        copies[-1].start()

    send(w1_s, w1_ref)
    send(b1_s, b1_ref)
    send(b2_s, b2_ref)
    for i in range(0, 64, 16):
        for j in range(6):
            w2_s[i : i + 16, j * 128 : (j + 1) * 128] = total_ref[j, i : i + 16].astype(F32)
        w2_s[i : i + 16, 768:864] = total_ref[6, i : i + 16].astype(F32)[:, :96]
        send(w2_s.at[pl.ds(i, 16)], w2_ref.at[pl.ds(i, 16)])
    for copy in copies:
        copy.wait()


def sum_everywhere(packed):
    vmem = pl.BlockSpec(memory_space=pltpu.VMEM)
    for axes in (("x", "c"), ("yh", "yl"), "z"):
        parts = lax.all_to_all(packed, axes, 0, 0, tiled=True)
        packed = pl.pallas_call(
            add_kernel,
            out_shape=jax.ShapeDtypeStruct(packed.shape, packed.dtype),
            in_specs=[vmem],
            out_specs=vmem,
            compiler_params=pltpu.CompilerParams(vmem_limit_bytes=8 * 2**20),
            name="add",
        )(parts)
    return lax.all_to_all(packed, ("x", "c"), 0, 0, tiled=True)


def local_step(volume, w1, b1, w2, b2, cotangent, space, count, cells):
    vol, cot = volume[0], cotangent[0]
    vmem, anywhere = pl.BlockSpec(memory_space=pltpu.VMEM), pl.BlockSpec(memory_space=pl.ANY)

    def edges(*refs):
        edges_kernel(space, *refs)

    to_pair, to_other = pl.pallas_call(
        edges,
        out_shape=(jax.ShapeDtypeStruct((4 * HALO + 16, 8, 256), BF16),) * 2,
        in_specs=[anywhere] * 2,
        out_specs=(vmem, vmem),
        scratch_shapes=[pltpu.VMEM((2, 64, 4, 128), BF16), pltpu.SemaphoreType.DMA((2, 5))],
        compiler_params=pltpu.CompilerParams(vmem_limit_bytes=8 * 2**20),
        name="edges",
    )(in_hbm(vol), in_hbm(cot))
    pairs = [(i, i ^ 1) for i in range(count)]
    others = [(i, i + 1) for i in range(1, count - 1, 2)] + [(i + 1, i) for i in range(1, count - 1, 2)]
    from_other = lax.ppermute(to_other, space, others)
    from_pair = lax.ppermute(to_pair, space, pairs)
    shapes = (
        ((256, 256), BF16),
        ((256, 1536), BF16),
        ((384, 768), BF16),
        ((256, 128), F32),
        ((256, 128), F32),
        ((256, 512), BF16),
        ((256, 128), F32),
        ((4, 256, 128), BF16),
        ((8, 160, 128), BF16),
        ((2, 4, 256, 128), BF16),
        ((2, 512, 128), BF16),
    )
    inputs = [in_hbm(x) for x in (vol, cot, w1, w2, b1.reshape(1, 32), b2.reshape(1, 64))]
    own = pl.pallas_call(
        own_kernel,
        out_shape=tuple(jax.ShapeDtypeStruct(*shape) for shape in shapes),
        in_specs=[anywhere] * 6,
        out_specs=(vmem,) * len(shapes),
        scratch_shapes=[
            *(pltpu.VMEM(x.shape, x.dtype) for x in inputs),
            pltpu.VMEM((16, 128), F32),
            pltpu.VMEM((8 * 128 + 8, 128), F32),
            pltpu.VMEM((1040, 128), F32),
            pltpu.VMEM((64, 1024), F32),
            pltpu.SemaphoreType.DMA((6,)),
        ],
        compiler_params=pltpu.CompilerParams(vmem_limit_bytes=16 * 2**20),
        cost_estimate=pl.CostEstimate(flops=500_000_000, bytes_accessed=4_000_000, transcendentals=0),
        name="own_planes",
    )(*inputs)

    def kernel(*refs):
        layers_kernel(
            *refs,
            space=space,
            last=count - 1,
            scale_first=1.0 / math.sqrt(cells),
            scale_second=1.0 / math.sqrt(cells / 8.0),
        )

    act, packed = pl.pallas_call(
        kernel,
        out_shape=(
            jax.ShapeDtypeStruct((64, 16, 128), BF16),
            jax.ShapeDtypeStruct((8, 64, 128), BF16),
        ),
        in_specs=[vmem] * (2 + len(shapes)),
        out_specs=(anywhere, vmem),
        scratch_shapes=[
            pltpu.VMEM((2, 4 * HALO + 16, 8, 256), BF16),
            pltpu.VMEM((2, HALO * 128 + 8, 128), F32),
            pltpu.VMEM((HALO, 160, 128), BF16),
            pltpu.VMEM((HALO, 160, 128), BF16),
            pltpu.VMEM((264, 128), F32),
            pltpu.VMEM((8, 512, 128), BF16),
            pltpu.VMEM((2, 4, 256, 128), BF16),
            pltpu.VMEM((6 * 256, 128), BF16),
            pltpu.VMEM((1040, 128), F32),
            pltpu.VMEM((64, 16, 128), BF16),
            pltpu.SemaphoreType.DMA,
        ],
        compiler_params=pltpu.CompilerParams(vmem_limit_bytes=32 * 2**20),
        cost_estimate=pl.CostEstimate(flops=2_500_000_000, bytes_accessed=4_000_000, transcendentals=0),
        name="layers",
    )(from_other, from_pair, *own)
    return act.reshape(1, 64, 4, 4, 128), packed


def solution(mesh):
    dp, space = mesh.shape["dp"], mesh.shape["space"]
    split = Mesh(mesh.devices.reshape(8, 2, 4, 4, 2), ("z", "yh", "x", "yl", "c"))
    along = ("x", "yl", "c")

    def on_device(volume, w1, b1, w2, b2, cotangent):
        cells = float(math.prod(volume.shape[2:]) * dp * space)
        act, packed = local_step(volume, w1, b1, w2, b2, cotangent, along, space, cells)
        total = sum_everywhere(packed)
        gw1, gb1, gw2, gb2 = pl.pallas_call(
            unpack_kernel,
            out_shape=(
                jax.ShapeDtypeStruct((32, 108), F32),
                jax.ShapeDtypeStruct((1, 32), F32),
                jax.ShapeDtypeStruct((64, 864), F32),
                jax.ShapeDtypeStruct((1, 64), F32),
            ),
            in_specs=[pl.BlockSpec(memory_space=pltpu.VMEM)],
            out_specs=(pl.BlockSpec(memory_space=pl.ANY),) * 4,
            scratch_shapes=[
                pltpu.VMEM((32, 108), F32),
                pltpu.VMEM((1, 32), F32),
                pltpu.VMEM((64, 864), F32),
                pltpu.VMEM((1, 64), F32),
                pltpu.SemaphoreType.DMA((7,)),
            ],
            compiler_params=pltpu.CompilerParams(vmem_limit_bytes=8 * 2**20),
            name="unpack",
        )(total)
        return act, gw1, gb1[0], gw2, gb2[0]

    shared = P(("z", "yh"), None, along, None, None)
    return jax.shard_map(
        on_device,
        mesh=split,
        in_specs=(shared, P(), P(), P(), P(), shared),
        out_specs=(shared, P(), P(), P(), P()),
        check_vma=False,
    )
```

```python
import math

import jax
import jax.numpy as jnp
import numpy as np
from jax import lax
from jax.experimental import pallas as pl
from jax.experimental.pallas import tpu as pltpu
from jax.sharding import Mesh, PartitionSpec as P

leak_slope = 0.3
F32, BF16 = jnp.float32, jnp.bfloat16
HALO = 5
NT = (((1,), (1,)), ((), ()))
BITS = ("z2", "z1", "z0", "y2", "x1", "x0", "y1", "y0", "c")
DP, SPACE = BITS[:4], BITS[4:]
CORES, Y, Z = ("x0", "x1", "c"), ("y0", "y1", "y2"), ("z0", "z1", "z2")


def edges_kernel(space, vol_ref, cot_ref, pair_ref, other_ref, cot_s, sems):
    second = lax.axis_index(space) % 2
    copies = []
    for side, ref, high in ((0, other_ref, second), (1, pair_ref, 1 - second)):
        copies.append(pltpu.make_async_copy(cot_ref.at[:, high * 3], cot_s.at[side], sems.at[side, 4]))
        for c in range(4):
            source = vol_ref.at[c, pl.ds(high * (8 - HALO), HALO)]
            copies.append(pltpu.make_async_copy(source, ref.at[pl.ds(c * HALO, HALO)], sems.at[side, c]))
    for copy in copies:
        copy.start()
    for copy in copies:
        copy.wait()
    for side, ref in ((0, other_ref), (1, pair_ref)):
        rows = cot_s[side].astype(F32).reshape(256, 128)
        rows = jnp.concatenate([rows[:128], rows[128:]], axis=1)
        ref[4 * HALO : 4 * HALO + 16] = rows.astype(BF16).reshape(16, 8, 256)


def add_kernel(parts_ref, out_ref):
    total = jnp.sum(parts_ref[...].astype(F32), axis=0).astype(BF16)
    for i in range(out_ref.shape[0]):
        out_ref[i] = total


def in_hbm(x):
    return pltpu.with_memory_space_constraint(x, pltpu.HBM)


def cell_shift(s):
    return (s // 2 % 2) * 64 + (s % 2) * 16 + (s // 4) * 4


def split_phases(rows, split, count, fine, win):
    parts = jnp.dot(rows, split, preferred_element_type=F32)
    for c in range(4):
        for x in range(count):
            for dz in range(4):
                fine[pl.ds(x * 128 + dz * 32 + c * 8, 8), :] = parts[
                    (c * count + x) * 8 : (c * count + x + 1) * 8, dz * 128 : (dz + 1) * 128
                ]
    for x in range(count):
        win[x, 0:16, :] = jnp.zeros((16, 128), BF16)
        win[x, 144:160, :] = jnp.zeros((16, 128), BF16)
        for y in range(8):
            win[x, (y + 1) * 16 : (y + 2) * 16, :] = fine[pl.ds(x * 128 + y, 16, stride=8), :].astype(BF16)


def window(planes, y):
    return jnp.concatenate([ref[x, 32 * y : 32 * y + 64, :] for ref, x in planes], axis=0)


def first_layer(planes, w1, bias, keep_pre, keep_pooled, mask):
    lane = lax.broadcasted_iota(jnp.int32, (32, 128), 1)
    for y0 in (0, 2):
        both = jnp.concatenate([window(planes, y0), window(planes, y0 + 1)], axis=1)
        pre = jnp.dot(w1, both, preferred_element_type=F32) + bias
        if keep_pre is not None:
            for i in range(2):
                keep_pre[y0 + i] = pre[:, i * 128 : (i + 1) * 128].astype(BF16)
        act = jnp.maximum(pre, leak_slope * pre)
        total = act[0:32]
        for s in range(1, 8):
            total = total + act[s * 32 : (s + 1) * 32]
        total = mask(total * 0.125)
        for i in range(2):
            pooled = total[:, i * 128 : (i + 1) * 128]
            at = (y0 + i) * 128
            keep_pooled[at : at + 32, :] = jnp.where(lane == 0, 0.0, pltpu.roll(pooled, 1, 1)).astype(BF16)
            keep_pooled[at + 32 : at + 64, :] = pooled.astype(BF16)
            keep_pooled[at + 64 : at + 96, :] = jnp.where(lane == 127, 0.0, pltpu.roll(pooled, 127, 1)).astype(BF16)
            keep_pooled[at + 96 : at + 128, :] = jnp.ones((32, 128), BF16)


def own_kernel(
    vol_hbm, cot_hbm, w1_hbm, w2_hbm, b1_hbm, b2_hbm,
    w1big_ref, wexp_ref, wt_ref, b1_ref, b2_ref, split_ref, compact_ref, cot_out, win, pre_out, pooled_out,
    vol_ref, cot_ref, w1_ref, w2_ref, b1_row, b2_row, rows8, fine, cot_s, w2_pad, sems,
):
    sources = (vol_hbm, w1_hbm, b1_hbm, b2_hbm, w2_hbm, cot_hbm)
    targets = (vol_ref, w1_ref, b1_row, b2_row, w2_ref, cot_ref)
    copies = [pltpu.make_async_copy(x, y, sems.at[i]) for i, (x, y) in enumerate(zip(sources, targets))]
    for copy in copies:
        copy.start()
    row = lax.broadcasted_iota(jnp.int32, (108, 256), 0)
    column = lax.broadcasted_iota(jnp.int32, (108, 256), 1)
    base = row // 36 * 64 + row // 12 % 3 * 16 + row % 12
    spread = jnp.where(column == base, 1.0, 0.0).astype(BF16)
    z = lax.broadcasted_iota(jnp.int32, (256, 128), 0)
    k = lax.broadcasted_iota(jnp.int32, (256, 128), 1)
    for dz in range(4):
        split_ref[:, dz * 128 : (dz + 1) * 128] = jnp.where(z == 2 * k - 1 + dz, 1.0, 0.0).astype(BF16)
    base = k // 36 * 64 + k // 12 % 3 * 16 + k % 12
    compact_ref[...] = jnp.where((z == base) & (k < 108), 1.0, 0.0)
    rows8[...] = jnp.zeros((16, 128), F32)
    w2_pad[...] = jnp.zeros((64, 1024), F32)
    for copy in copies[:4]:
        copy.wait()

    wide = jnp.dot(w1_ref[...], spread, preferred_element_type=F32)
    for s in range(8):
        shift = cell_shift(s)
        moved = pltpu.roll(wide, shift, 1) if shift else wide
        w1big_ref[s * 32 : (s + 1) * 32, :] = moved.astype(BF16)
    rows8[0:1, 0:32] = b1_row[...]
    rows8[8:9, 0:64] = b2_row[...]
    b1 = jnp.broadcast_to(rows8[0:1, :], (128, 128)).T[:32]
    b1_ref[...] = jnp.concatenate([b1] * 8, axis=0)
    b2 = jnp.broadcast_to(rows8[8:9, :], (128, 128)).T[:64]
    b2_ref[...] = jnp.concatenate([b2] * 4, axis=0)

    rows = vol_ref[...].astype(F32).reshape(256, 256).astype(BF16)
    split_phases(rows, split_ref[...], 8, fine, win)
    bias = b1_ref[...]
    bias = jnp.concatenate([bias, bias], axis=1)
    for i in range(2):
        planes = [(win, 1 + 2 * i + dx) for dx in range(4)]
        first_layer(planes, w1big_ref[...], bias, pre_out.at[i], pooled_out.at[i], lambda v: v)

    copies[4].wait()
    w2_pad[:, 0:864] = w2_ref[...].astype(F32)
    lane = lax.broadcasted_iota(jnp.int32, (64, 128), 1)
    zero = jnp.zeros((64, 128), F32)
    units = []
    for u in range(9):
        start = 96 * u // 128 * 128
        part = w2_pad[:, start : start + 256]
        if 96 * u > start:
            part = pltpu.roll(part, 256 - (96 * u - start), 1)
        units.append(jnp.where(lane < 96, part[:, :128], 0.0))
    for dx in range(3):
        for yin in range(4):
            at = (dx * 4 + yin) * 128
            rows = []
            for y in range(4):
                dy = yin - y + 1
                rows.append(units[dx * 3 + dy] if 0 <= dy <= 2 else zero)
            for pair in range(2):
                block = jnp.concatenate(rows[2 * pair : 2 * pair + 2], axis=0)
                wexp_ref[pair * 128 : (pair + 1) * 128, at : at + 128] = block.astype(BF16)
                col = (2 - dx) * 256 + pair * 128
                wt_ref[yin * 96 : (yin + 1) * 96, col : col + 128] = block.T[:96].astype(BF16)

    copies[5].wait()
    cot_s[0:1024, :] = cot_ref[...].astype(F32).reshape(1024, 128)
    for p in range(4):
        for y in range(4):
            cot_out[p, y * 64 : (y + 1) * 64, :] = cot_s[pl.ds(p * 4 + y, 64, stride=16), :].astype(BF16)


def layers_kernel(
    other_ref, pair_ref,
    w1_ref, wexp_ref, wt_ref, b1_ref, b2_ref, split_ref, compact_ref, cot_ref, win, pre_own, pooled_own,
    act_ref, grad_ref,
    halo, fine, win_low, win_high, cot_s, ps, pre_s, g2s, act_s, act_out, sem,
    *, space, last, scale_first, scale_second,
):
    place = lax.axis_index(space)
    second = place % 2

    @pl.when(second == 0)
    def _():
        halo[0] = other_ref[...]
        halo[1] = pair_ref[...]

    @pl.when(second != 0)
    def _():
        halo[0] = pair_ref[...]
        halo[1] = other_ref[...]

    for side, target in ((0, win_low), (1, win_high)):
        rows = halo[side, 0 : 4 * HALO].astype(F32).reshape(160, 256).astype(BF16)
        split_phases(rows, split_ref[...], HALO, fine.at[side], target)

    def plane(x):
        if x < HALO:
            return win_low, x
        if x < HALO + 8:
            return win, x - HALO
        return win_high, x - HALO - 8

    bias1 = b1_ref[...]
    bias1 = jnp.concatenate([bias1, bias1], axis=1)
    bias2 = b2_ref[...]
    bias2 = jnp.concatenate([bias2, bias2], axis=1)
    for q in (0, 1, 2, 5, 6, 7):
        keep = pre_s.at[0] if q == 2 else pre_s.at[1] if q == 5 else None
        if q < 2:
            mask = lambda v: jnp.where(place > 0, v, 0.0)
        elif q > 5:
            mask = lambda v: jnp.where(place < last, v, 0.0)
        else:
            mask = lambda v: v
        first_layer([plane(2 * q + dx) for dx in range(4)], w1_ref[...], bias1, keep, ps.at[q], mask)

    def pooled(q):
        return pooled_own[q - 3] if q in (3, 4) else ps[q]

    def three(r):
        return jnp.concatenate([pooled(r), pooled(r + 1), pooled(r + 2)], axis=0)

    both = jnp.concatenate([three(r) for r in range(6)], axis=1)
    pre = jnp.dot(wexp_ref[...], both, preferred_element_type=F32) + jnp.concatenate([bias2] * 3, axis=1)
    act = jnp.maximum(pre, leak_slope * pre)
    for r in range(6):
        if 1 <= r <= 4:
            cot = cot_ref[r - 1].astype(F32)
            for y in range(4):
                act_s[pl.ds((r - 1) * 4 + y, 64, stride=16), :] = act[
                    y * 64 : (y + 1) * 64, r * 128 : (r + 1) * 128
                ]
        else:
            sent = halo[r // 5, 4 * HALO : 4 * HALO + 16].astype(F32).reshape(128, 256)
            cot_s[0:128, :] = sent[:, 0:128]
            cot_s[128:256, :] = sent[:, 128:256]
            cot = jnp.concatenate([cot_s[pl.ds(y, 64, stride=4), :] for y in range(4)], axis=0)
        own = pre[:, r * 128 : (r + 1) * 128]
        g2s[r * 256 : (r + 1) * 256, :] = jnp.where(own > 0, cot, leak_slope * cot).astype(BF16)
    act_out[...] = act_s[0:1024, :].reshape(64, 16, 128).astype(BF16)
    copy = pltpu.make_async_copy(act_out, act_ref, sem)
    copy.start()

    lane = lax.broadcasted_iota(jnp.int32, (32, 128), 1)
    ones = jnp.ones((8, 512), BF16)
    all_cells, all_cols = [], []
    q = jnp.dot(
        wt_ref[...],
        jnp.concatenate([g2s[p * 256 : (p + 3) * 256, :] for p in range(4)], axis=1),
        preferred_element_type=F32,
    )
    for p in range(4):
        pre_p = pre_own.at[p - 1] if p in (1, 2) else pre_s.at[p // 3]
        cells = []
        for y in range(4):
            taps = q[y * 96 : (y + 1) * 96, p * 128 : (p + 1) * 128] * 0.125
            g = (
                jnp.where(lane == 127, 0.0, pltpu.roll(taps[0:32], 127, 1))
                + taps[32:64]
                + jnp.where(lane == 0, 0.0, pltpu.roll(taps[64:96], 1, 1))
            )
            low = leak_slope * g
            pre = pre_p[y].astype(F32)
            cells.append(
                jnp.concatenate(
                    [jnp.where(pre[s * 32 : (s + 1) * 32] > 0, g, low) for s in range(8)], axis=0
                ).astype(BF16)
            )
        planes = [plane(2 * (p + 2) + dx) for dx in range(4)]
        cols = jnp.concatenate([window(planes, y) for y in range(4)], axis=1)
        cols = jnp.concatenate([cols, ones], axis=0)
        all_cells.append(jnp.concatenate(cells, axis=1))
        all_cols.append(cols)
    m1 = lax.dot_general(
        jnp.concatenate(all_cells, axis=1), jnp.concatenate(all_cols, axis=1), NT, preferred_element_type=F32
    )

    lane96 = lax.broadcasted_iota(jnp.int32, (96, 128), 1)
    grads = jnp.concatenate([g2s[(p + 1) * 256 : (p + 2) * 256, :] for p in range(4)], axis=1)
    folded = []
    b2_grad = None
    cols = jnp.concatenate([jnp.concatenate([pooled(p + 1 + dx) for p in range(4)], axis=1) for dx in range(3)], axis=0)
    tt = lax.dot_general(cols, grads, NT, preferred_element_type=F32)
    for dx in range(3):
        t = tt[dx * 512 : (dx + 1) * 512]
        if dx == 0:
            b2_grad = t[96:104, 0:128] + t[96:104, 128:256]
        for dy in range(3):
            sums = []
            for parity in range(2):
                total = None
                for y in (parity, parity + 2):
                    yin = y + dy - 1
                    if 0 <= yin < 4:
                        piece = t[yin * 128 : yin * 128 + 96, (y // 2) * 128 : (y // 2 + 1) * 128]
                        total = piece if total is None else total + piece
                sums.append(total)
            u = jnp.where(lane96 < 64, sums[0], sums[1])
            folded.append(u + pltpu.roll(u, 64, 1))
    folded = jnp.concatenate(folded + [jnp.zeros((160, 128), F32)], axis=0) * scale_second
    lane128 = lax.broadcasted_iota(jnp.int32, (128, 128), 1)
    for j in range(0, 8, 2):
        two = jnp.where(lane128 < 64, folded[j * 128 : (j + 1) * 128], folded[(j + 1) * 128 : (j + 2) * 128]).T
        grad_ref[j] = two[:64].astype(BF16)
        if j < 6:
            grad_ref[j + 1] = two[64:].astype(BF16)

    total = m1[0:32, 0:256]
    for s in range(1, 8):
        total = total + pltpu.roll(m1[s * 32 : (s + 1) * 32, 0:256], 256 - cell_shift(s), 1)
    w1_grad = jnp.dot(total, compact_ref[...], precision=lax.Precision.HIGHEST, preferred_element_type=F32)
    sums = m1[0:32, 256:257]
    for s in range(1, 8):
        sums = sums + m1[s * 32 : (s + 1) * 32, 256:257]
    b1_grad = jnp.concatenate([jnp.broadcast_to(sums, (32, 128)), jnp.zeros((96, 128), F32)], axis=0).T[:8]
    b2_grad = b2_grad + pltpu.roll(b2_grad, 64, 1)
    biases = jnp.concatenate([b1_grad * scale_first, b2_grad * scale_second], axis=0)
    grad_ref[7, 0:32, :] = (w1_grad * scale_first).astype(BF16)
    grad_ref[7, 32:48, :] = biases.astype(BF16)
    grad_ref[7, 48:64, :] = jnp.zeros((16, 128), BF16)
    copy.wait()


def unpack_kernel(total_ref, w1_ref, b1_ref, w2_ref, b2_ref, w1_s, b1_s, w2_s, b2_s, sems):
    rest = total_ref[7].astype(F32)
    w1_s[...] = rest[0:32, 0:108]
    b1_s[...] = rest[32:33, 0:32]
    b2_s[...] = rest[40:41, 0:64]
    copies = []

    def send(source, target):
        copies.append(pltpu.make_async_copy(source, target, sems.at[len(copies)]))
        copies[-1].start()

    send(w1_s, w1_ref)
    send(b1_s, b1_ref)
    send(b2_s, b2_ref)
    for i in range(0, 64, 16):
        for j in range(6):
            w2_s[i : i + 16, j * 128 : (j + 1) * 128] = total_ref[j, i : i + 16].astype(F32)
        w2_s[i : i + 16, 768:864] = total_ref[6, i : i + 16].astype(F32)[:, :96]
        send(w2_s.at[pl.ds(i, 16)], w2_ref.at[pl.ds(i, 16)])
    for copy in copies:
        copy.wait()


def sum_everywhere(packed):
    vmem = pl.BlockSpec(memory_space=pltpu.VMEM)
    for axes in (CORES, Y, Z):
        parts = lax.all_to_all(packed, axes, 0, 0, tiled=True)
        packed = pl.pallas_call(
            add_kernel,
            out_shape=jax.ShapeDtypeStruct(packed.shape, packed.dtype),
            in_specs=[vmem],
            out_specs=vmem,
            compiler_params=pltpu.CompilerParams(vmem_limit_bytes=8 * 2**20),
            name="add",
        )(parts)
    return lax.all_to_all(packed, CORES, 0, 0, tiled=True)


def local_step(volume, w1, b1, w2, b2, cotangent, space, count, cells):
    vol, cot = volume[0], cotangent[0]
    vmem, anywhere = pl.BlockSpec(memory_space=pltpu.VMEM), pl.BlockSpec(memory_space=pl.ANY)

    def edges(*refs):
        edges_kernel(space, *refs)

    to_pair, to_other = pl.pallas_call(
        edges,
        out_shape=(jax.ShapeDtypeStruct((4 * HALO + 16, 8, 256), BF16),) * 2,
        in_specs=[anywhere] * 2,
        out_specs=(vmem, vmem),
        scratch_shapes=[pltpu.VMEM((2, 64, 4, 128), BF16), pltpu.SemaphoreType.DMA((2, 5))],
        compiler_params=pltpu.CompilerParams(vmem_limit_bytes=8 * 2**20),
        name="edges",
    )(in_hbm(vol), in_hbm(cot))
    pairs = [(i, i ^ 1) for i in range(count)]
    others = [(i, i + 1) for i in range(1, count - 1, 2)] + [(i + 1, i) for i in range(1, count - 1, 2)]
    from_other = lax.ppermute(to_other, space, others)
    from_pair = lax.ppermute(to_pair, space, pairs)
    shapes = (
        ((256, 256), BF16),
        ((256, 1536), BF16),
        ((384, 768), BF16),
        ((256, 128), F32),
        ((256, 128), F32),
        ((256, 512), BF16),
        ((256, 128), F32),
        ((4, 256, 128), BF16),
        ((8, 160, 128), BF16),
        ((2, 4, 256, 128), BF16),
        ((2, 512, 128), BF16),
    )
    inputs = [in_hbm(x) for x in (vol, cot, w1, w2, b1.reshape(1, 32), b2.reshape(1, 64))]
    own = pl.pallas_call(
        own_kernel,
        out_shape=tuple(jax.ShapeDtypeStruct(*shape) for shape in shapes),
        in_specs=[anywhere] * 6,
        out_specs=(vmem,) * len(shapes),
        scratch_shapes=[
            *(pltpu.VMEM(x.shape, x.dtype) for x in inputs),
            pltpu.VMEM((16, 128), F32),
            pltpu.VMEM((8 * 128 + 8, 128), F32),
            pltpu.VMEM((1040, 128), F32),
            pltpu.VMEM((64, 1024), F32),
            pltpu.SemaphoreType.DMA((6,)),
        ],
        compiler_params=pltpu.CompilerParams(vmem_limit_bytes=16 * 2**20),
        cost_estimate=pl.CostEstimate(flops=500_000_000, bytes_accessed=4_000_000, transcendentals=0),
        name="own_planes",
    )(*inputs)

    def kernel(*refs):
        layers_kernel(
            *refs,
            space=space,
            last=count - 1,
            scale_first=1.0 / math.sqrt(cells),
            scale_second=1.0 / math.sqrt(cells / 8.0),
        )

    act, packed = pl.pallas_call(
        kernel,
        out_shape=(
            jax.ShapeDtypeStruct((64, 16, 128), BF16),
            jax.ShapeDtypeStruct((8, 64, 128), BF16),
        ),
        in_specs=[vmem] * (2 + len(shapes)),
        out_specs=(anywhere, vmem),
        scratch_shapes=[
            pltpu.VMEM((2, 4 * HALO + 16, 8, 256), BF16),
            pltpu.VMEM((2, HALO * 128 + 8, 128), F32),
            pltpu.VMEM((HALO, 160, 128), BF16),
            pltpu.VMEM((HALO, 160, 128), BF16),
            pltpu.VMEM((264, 128), F32),
            pltpu.VMEM((8, 512, 128), BF16),
            pltpu.VMEM((2, 4, 256, 128), BF16),
            pltpu.VMEM((6 * 256, 128), BF16),
            pltpu.VMEM((1040, 128), F32),
            pltpu.VMEM((64, 16, 128), BF16),
            pltpu.SemaphoreType.DMA,
        ],
        compiler_params=pltpu.CompilerParams(vmem_limit_bytes=32 * 2**20),
        cost_estimate=pl.CostEstimate(flops=2_500_000_000, bytes_accessed=4_000_000, transcendentals=0),
        name="layers",
    )(from_other, from_pair, *own)
    return act.reshape(1, 64, 4, 4, 128), packed


def solution(mesh):
    dp, space = mesh.shape["dp"], mesh.shape["space"]
    split = Mesh(mesh.devices.reshape((2,) * 9), BITS)

    def on_device(volume, w1, b1, w2, b2, cotangent):
        cells = float(math.prod(volume.shape[2:]) * dp * space)
        act, packed = local_step(volume, w1, b1, w2, b2, cotangent, SPACE, space, cells)
        total = sum_everywhere(packed)
        gw1, gb1, gw2, gb2 = pl.pallas_call(
            unpack_kernel,
            out_shape=(
                jax.ShapeDtypeStruct((32, 108), F32),
                jax.ShapeDtypeStruct((1, 32), F32),
                jax.ShapeDtypeStruct((64, 864), F32),
                jax.ShapeDtypeStruct((1, 64), F32),
            ),
            in_specs=[pl.BlockSpec(memory_space=pltpu.VMEM)],
            out_specs=(pl.BlockSpec(memory_space=pl.ANY),) * 4,
            scratch_shapes=[
                pltpu.VMEM((32, 108), F32),
                pltpu.VMEM((1, 32), F32),
                pltpu.VMEM((64, 864), F32),
                pltpu.VMEM((1, 64), F32),
                pltpu.SemaphoreType.DMA((7,)),
            ],
            compiler_params=pltpu.CompilerParams(vmem_limit_bytes=8 * 2**20),
            name="unpack",
        )(total)
        return act, gw1, gb1[0], gw2, gb2[0]

    shared = P(DP, None, SPACE, None, None)
    return jax.shard_map(
        on_device,
        mesh=split,
        in_specs=(shared, P(), P(), P(), P(), shared),
        out_specs=(shared, P(), P(), P(), P()),
        check_vma=False,
    )
```

```python
import math

import jax
import jax.numpy as jnp
import numpy as np
from jax import lax
from jax.experimental import pallas as pl
from jax.experimental.pallas import tpu as pltpu
from jax.sharding import Mesh, PartitionSpec as P

leak_slope = 0.3
F32, BF16 = jnp.float32, jnp.bfloat16
HALO = 5
NT = (((1,), (1,)), ((), ()))
BITS = ("z2", "z1", "z0", "y2", "x1", "x0", "y1", "y0", "c")
DP, SPACE = BITS[:4], BITS[4:]
CORES, Y, Z = ("x0", "x1", "c"), ("y0", "y1", "y2"), ("z0", "z1", "z2")


def edges_kernel(
    space, vol_hbm, cot_hbm, pair_ref, other_ref, split_ref, compact_ref, spread_ref, cot_s, sems
):
    second = lax.axis_index(space) % 2
    copies = []
    for side, ref, high in ((0, other_ref, second), (1, pair_ref, 1 - second)):
        copies.append(pltpu.make_async_copy(cot_hbm.at[:, high * 3], cot_s.at[side], sems.at[side, 4]))
        for c in range(4):
            source = vol_hbm.at[c, pl.ds(high * (8 - HALO), HALO)]
            copies.append(pltpu.make_async_copy(source, ref.at[pl.ds(c * HALO, HALO)], sems.at[side, c]))
    for copy in copies:
        copy.start()

    z = lax.broadcasted_iota(jnp.int32, (256, 128), 0)
    k = lax.broadcasted_iota(jnp.int32, (256, 128), 1)
    for dz in range(4):
        split_ref[:, dz * 128 : (dz + 1) * 128] = jnp.where(z == 2 * k - 1 + dz, 1.0, 0.0).astype(BF16)
    base = k // 36 * 64 + k // 12 % 3 * 16 + k % 12
    compact_ref[...] = jnp.where((z == base) & (k < 108), 1.0, 0.0)
    row = lax.broadcasted_iota(jnp.int32, (108, 256), 0)
    column = lax.broadcasted_iota(jnp.int32, (108, 256), 1)
    base = row // 36 * 64 + row // 12 % 3 * 16 + row % 12
    spread_ref[...] = jnp.where(column == base, 1.0, 0.0).astype(BF16)

    for copy in copies:
        copy.wait()
    for side, ref in ((0, other_ref), (1, pair_ref)):
        rows = cot_s[side].astype(F32).reshape(256, 128)
        rows = jnp.concatenate([rows[:128], rows[128:]], axis=1)
        ref[4 * HALO : 4 * HALO + 16] = rows.astype(BF16).reshape(16, 8, 256)


def add_kernel(parts_ref, out_ref):
    total = jnp.sum(parts_ref[...].astype(F32), axis=0).astype(BF16)
    for i in range(out_ref.shape[0]):
        out_ref[i] = total


def in_hbm(x):
    return pltpu.with_memory_space_constraint(x, pltpu.HBM)


def cell_shift(s):
    return (s // 2 % 2) * 64 + (s % 2) * 16 + (s // 4) * 4


def split_phases(rows, split, count, fine, win):
    parts = jnp.dot(rows, split, preferred_element_type=F32)
    for c in range(4):
        for x in range(count):
            for dz in range(4):
                fine[pl.ds(x * 128 + dz * 32 + c * 8, 8), :] = parts[
                    (c * count + x) * 8 : (c * count + x + 1) * 8, dz * 128 : (dz + 1) * 128
                ]
    for x in range(count):
        win[x, 0:16, :] = jnp.zeros((16, 128), BF16)
        win[x, 144:160, :] = jnp.zeros((16, 128), BF16)
        for y in range(8):
            win[x, (y + 1) * 16 : (y + 2) * 16, :] = fine[pl.ds(x * 128 + y, 16, stride=8), :].astype(BF16)


def window(planes, y):
    return jnp.concatenate([ref[x, 32 * y : 32 * y + 64, :] for ref, x in planes], axis=0)


def first_layer(planes, w1, bias, keep_pre, keep_pooled, mask):
    lane = lax.broadcasted_iota(jnp.int32, (32, 128), 1)
    for y0 in (0, 2):
        both = jnp.concatenate([window(planes, y0), window(planes, y0 + 1)], axis=1)
        pre = jnp.dot(w1, both, preferred_element_type=F32) + bias
        if keep_pre is not None:
            for i in range(2):
                keep_pre[y0 + i] = pre[:, i * 128 : (i + 1) * 128].astype(BF16)
        act = jnp.maximum(pre, leak_slope * pre)
        total = act[0:32]
        for s in range(1, 8):
            total = total + act[s * 32 : (s + 1) * 32]
        total = mask(total * 0.125)
        for i in range(2):
            pooled = total[:, i * 128 : (i + 1) * 128]
            at = (y0 + i) * 96
            keep_pooled[at : at + 32, :] = jnp.where(lane == 0, 0.0, pltpu.roll(pooled, 1, 1)).astype(BF16)
            keep_pooled[at + 32 : at + 64, :] = pooled.astype(BF16)
            keep_pooled[at + 64 : at + 96, :] = jnp.where(lane == 127, 0.0, pltpu.roll(pooled, 127, 1)).astype(BF16)


def own_kernel(
    vol_hbm, w1_hbm, b1_hbm, b2_hbm, w2_hbm, cot_hbm, split_ref, spread_ref,
    w1big_ref, wexp_ref, wt_ref, b1_ref, b2_ref, cot_out, win, pre_out, pooled_out,
    vol_ref, w1_ref, b1_row, b2_row, w2_ref, cot_ref, rows8, fine, cot_s, w2_pad, sems,
):
    sources = (vol_hbm, w1_hbm, b1_hbm, b2_hbm, w2_hbm, cot_hbm)
    targets = (vol_ref, w1_ref, b1_row, b2_row, w2_ref, cot_ref)
    copies = [pltpu.make_async_copy(x, y, sems.at[i]) for i, (x, y) in enumerate(zip(sources, targets))]
    for copy in copies:
        copy.start()
    rows8[...] = jnp.zeros((16, 128), F32)
    w2_pad[...] = jnp.zeros((64, 1024), F32)
    for copy in copies:
        copy.wait()

    wide = jnp.dot(w1_ref[...], spread_ref[...], preferred_element_type=F32)
    for s in range(8):
        shift = cell_shift(s)
        moved = pltpu.roll(wide, shift, 1) if shift else wide
        w1big_ref[s * 32 : (s + 1) * 32, :] = moved.astype(BF16)
    rows8[0:1, 0:32] = b1_row[...]
    rows8[8:9, 0:64] = b2_row[...]
    b1 = jnp.broadcast_to(rows8[0:1, :], (128, 128)).T[:32]
    b1_ref[...] = jnp.concatenate([b1] * 8, axis=0)
    b2 = jnp.broadcast_to(rows8[8:9, :], (128, 128)).T[:64]
    b2_ref[...] = jnp.concatenate([b2] * 4, axis=0)

    rows = vol_ref[...].astype(F32).reshape(256, 256).astype(BF16)
    split_phases(rows, split_ref[...], 8, fine, win)
    bias = b1_ref[...]
    bias = jnp.concatenate([bias, bias], axis=1)
    for i in range(2):
        planes = [(win, 1 + 2 * i + dx) for dx in range(4)]
        first_layer(planes, w1big_ref[...], bias, pre_out.at[i], pooled_out.at[i], lambda v: v)

    w2_pad[:, 0:864] = w2_ref[...].astype(F32)
    lane = lax.broadcasted_iota(jnp.int32, (64, 512), 1)
    for dx in range(3):
        start = dx * 288 // 128 * 128
        taps = w2_pad[:, start : start + 512]
        rows = []
        for y in range(4):
            at = 96 * (y - 1)
            shift = (at - (dx * 288 - start)) % 512
            moved = pltpu.roll(taps, shift, 1) if shift else taps
            rows.append(jnp.where((lane >= max(at, 0)) & (lane < min(at + 288, 384)), moved, 0.0)[:, :384])
        for pair in range(2):
            block = jnp.concatenate(rows[2 * pair : 2 * pair + 2], axis=0)
            wexp_ref[pair * 128 : (pair + 1) * 128, dx * 384 : (dx + 1) * 384] = block.astype(BF16)
            col = (2 - dx) * 256 + pair * 128
            wt_ref[:, col : col + 128] = block.T.astype(BF16)

    cot_s[0:1024, :] = cot_ref[...].astype(F32).reshape(1024, 128)
    for p in range(4):
        for y in range(4):
            cot_out[p, y * 64 : (y + 1) * 64, :] = cot_s[pl.ds(p * 4 + y, 64, stride=16), :].astype(BF16)


def layers_kernel(
    other_ref, pair_ref,
    split_ref, compact_ref, w1_ref, wexp_ref, wt_ref, b1_ref, b2_ref, cot_ref, win, pre_own, pooled_own,
    act_ref, grad_ref,
    fine, win_low, win_high, cot_s, ps, pre_s, g2s, act_s, act_out, sem,
    *, space, last, scale_first, scale_second,
):
    place = lax.axis_index(space)
    second = place % 2

    def side(low, start, stop):
        first, other = (other_ref, pair_ref) if low else (pair_ref, other_ref)
        return jnp.where(second == 0, first[start:stop].astype(F32), other[start:stop].astype(F32))

    for low, target in ((True, win_low), (False, win_high)):
        rows = side(low, 0, 4 * HALO).reshape(160, 256).astype(BF16)
        split_phases(rows, split_ref[...], HALO, fine.at[1 - low], target)

    def plane(x):
        if x < HALO:
            return win_low, x
        if x < HALO + 8:
            return win, x - HALO
        return win_high, x - HALO - 8

    bias1 = b1_ref[...]
    bias1 = jnp.concatenate([bias1, bias1], axis=1)
    bias2 = b2_ref[...]
    bias2 = jnp.concatenate([bias2, bias2], axis=1)
    for q in (0, 1, 2, 5, 6, 7):
        keep = pre_s.at[0] if q == 2 else pre_s.at[1] if q == 5 else None
        if q < 2:
            mask = lambda v: jnp.where(place > 0, v, 0.0)
        elif q > 5:
            mask = lambda v: jnp.where(place < last, v, 0.0)
        else:
            mask = lambda v: v
        first_layer([plane(2 * q + dx) for dx in range(4)], w1_ref[...], bias1, keep, ps.at[q], mask)

    def pooled(q):
        return pooled_own[q - 3] if q in (3, 4) else ps[q]

    def three(r):
        return jnp.concatenate([pooled(r), pooled(r + 1), pooled(r + 2)], axis=0)

    both = jnp.concatenate([three(r) for r in range(6)], axis=1)
    pre = jnp.dot(wexp_ref[...], both, preferred_element_type=F32) + jnp.concatenate([bias2] * 3, axis=1)
    act = jnp.maximum(pre, leak_slope * pre)
    for r in range(6):
        if 1 <= r <= 4:
            cot = cot_ref[r - 1].astype(F32)
            for y in range(4):
                act_s[pl.ds((r - 1) * 4 + y, 64, stride=16), :] = act[
                    y * 64 : (y + 1) * 64, r * 128 : (r + 1) * 128
                ]
        else:
            sent = side(r == 0, 4 * HALO, 4 * HALO + 16).reshape(128, 256)
            cot_s[0:128, :] = sent[:, 0:128]
            cot_s[128:256, :] = sent[:, 128:256]
            cot = jnp.concatenate([cot_s[pl.ds(y, 64, stride=4), :] for y in range(4)], axis=0)
        own = pre[:, r * 128 : (r + 1) * 128]
        g2s[r * 256 : (r + 1) * 256, :] = jnp.where(own > 0, cot, leak_slope * cot).astype(BF16)
    act_out[...] = act_s[0:1024, :].reshape(64, 16, 128).astype(BF16)
    copy = pltpu.make_async_copy(act_out, act_ref, sem)
    copy.start()

    lane = lax.broadcasted_iota(jnp.int32, (32, 128), 1)
    ones = jnp.ones((8, 512), BF16)
    all_cells, all_cols = [], []
    q = jnp.dot(
        wt_ref[...],
        jnp.concatenate([g2s[p * 256 : (p + 3) * 256, :] for p in range(4)], axis=1),
        preferred_element_type=F32,
    )
    for p in range(4):
        pre_p = pre_own.at[p - 1] if p in (1, 2) else pre_s.at[p // 3]
        cells = []
        for y in range(4):
            taps = q[y * 96 : (y + 1) * 96, p * 128 : (p + 1) * 128] * 0.125
            g = (
                jnp.where(lane == 127, 0.0, pltpu.roll(taps[0:32], 127, 1))
                + taps[32:64]
                + jnp.where(lane == 0, 0.0, pltpu.roll(taps[64:96], 1, 1))
            )
            low = leak_slope * g
            pre = pre_p[y].astype(F32)
            cells.append(
                jnp.concatenate(
                    [jnp.where(pre[s * 32 : (s + 1) * 32] > 0, g, low) for s in range(8)], axis=0
                ).astype(BF16)
            )
        planes = [plane(2 * (p + 2) + dx) for dx in range(4)]
        cols = jnp.concatenate([window(planes, y) for y in range(4)], axis=1)
        cols = jnp.concatenate([cols, ones], axis=0)
        all_cells.append(jnp.concatenate(cells, axis=1))
        all_cols.append(cols)
    m1 = lax.dot_general(
        jnp.concatenate(all_cells, axis=1), jnp.concatenate(all_cols, axis=1), NT, preferred_element_type=F32
    )

    lane96 = lax.broadcasted_iota(jnp.int32, (96, 128), 1)
    grads = jnp.concatenate([g2s[(p + 1) * 256 : (p + 2) * 256, :] for p in range(4)], axis=1)
    folded = []
    cols = [jnp.concatenate([pooled(p + 1 + dx) for p in range(4)], axis=1) for dx in range(3)]
    tt = lax.dot_general(jnp.concatenate(cols + [ones], axis=0), grads, NT, preferred_element_type=F32)
    b2_grad = tt[1152:1160, 0:128] + tt[1152:1160, 128:256]
    for dx in range(3):
        t = tt[dx * 384 : (dx + 1) * 384]
        for dy in range(3):
            sums = []
            for parity in range(2):
                total = None
                for y in (parity, parity + 2):
                    yin = y + dy - 1
                    if 0 <= yin < 4:
                        piece = t[yin * 96 : (yin + 1) * 96, (y // 2) * 128 : (y // 2 + 1) * 128]
                        total = piece if total is None else total + piece
                sums.append(total)
            u = jnp.where(lane96 < 64, sums[0], sums[1])
            folded.append(u + pltpu.roll(u, 64, 1))
    folded = jnp.concatenate(folded + [jnp.zeros((160, 128), F32)], axis=0) * scale_second
    lane128 = lax.broadcasted_iota(jnp.int32, (128, 128), 1)
    for j in range(0, 8, 2):
        two = jnp.where(lane128 < 64, folded[j * 128 : (j + 1) * 128], folded[(j + 1) * 128 : (j + 2) * 128]).T
        grad_ref[j] = two[:64].astype(BF16)
        if j < 6:
            grad_ref[j + 1] = two[64:].astype(BF16)

    total = m1[0:32, 0:256]
    for s in range(1, 8):
        total = total + pltpu.roll(m1[s * 32 : (s + 1) * 32, 0:256], 256 - cell_shift(s), 1)
    w1_grad = jnp.dot(total, compact_ref[...], precision=lax.Precision.HIGHEST, preferred_element_type=F32)
    sums = m1[0:32, 256:257]
    for s in range(1, 8):
        sums = sums + m1[s * 32 : (s + 1) * 32, 256:257]
    b1_grad = jnp.concatenate([jnp.broadcast_to(sums, (32, 128)), jnp.zeros((96, 128), F32)], axis=0).T[:8]
    b2_grad = b2_grad + pltpu.roll(b2_grad, 64, 1)
    biases = jnp.concatenate([b1_grad * scale_first, b2_grad * scale_second], axis=0)
    grad_ref[7, 0:32, :] = (w1_grad * scale_first).astype(BF16)
    grad_ref[7, 32:48, :] = biases.astype(BF16)
    grad_ref[7, 48:64, :] = jnp.zeros((16, 128), BF16)
    copy.wait()


def unpack_kernel(total_ref, w1_ref, b1_ref, w2_ref, b2_ref, w1_s, b1_s, w2_s, b2_s, sems):
    rest = total_ref[7].astype(F32)
    w1_s[...] = rest[0:32, 0:108]
    b1_s[...] = rest[32:33, 0:32]
    b2_s[...] = rest[40:41, 0:64]
    copies = []

    def send(source, target):
        copies.append(pltpu.make_async_copy(source, target, sems.at[len(copies)]))
        copies[-1].start()

    send(w1_s, w1_ref)
    send(b1_s, b1_ref)
    send(b2_s, b2_ref)
    for i in range(0, 64, 16):
        for j in range(6):
            w2_s[i : i + 16, j * 128 : (j + 1) * 128] = total_ref[j, i : i + 16].astype(F32)
        w2_s[i : i + 16, 768:864] = total_ref[6, i : i + 16].astype(F32)[:, :96]
        send(w2_s.at[pl.ds(i, 16)], w2_ref.at[pl.ds(i, 16)])
    for copy in copies:
        copy.wait()


def sum_everywhere(packed):
    vmem = pl.BlockSpec(memory_space=pltpu.VMEM)
    for axes in (CORES, Y, Z):
        parts = lax.all_to_all(packed, axes, 0, 0, tiled=True)
        packed = pl.pallas_call(
            add_kernel,
            out_shape=jax.ShapeDtypeStruct(packed.shape, packed.dtype),
            in_specs=[vmem],
            out_specs=vmem,
            compiler_params=pltpu.CompilerParams(vmem_limit_bytes=8 * 2**20),
            name="add",
        )(parts)
    return lax.all_to_all(packed, CORES, 0, 0, tiled=True)


def local_step(volume, w1, b1, w2, b2, cotangent, space, count, cells):
    vol, cot = volume[0], cotangent[0]
    vmem, anywhere = pl.BlockSpec(memory_space=pltpu.VMEM), pl.BlockSpec(memory_space=pl.ANY)

    def edges(*refs):
        edges_kernel(space, *refs)

    inputs = [in_hbm(x) for x in (vol, w1, b1.reshape(1, 32), b2.reshape(1, 64), w2, cot)]
    message = jax.ShapeDtypeStruct((4 * HALO + 16, 8, 256), BF16)
    to_pair, to_other, split, compact, spread = pl.pallas_call(
        edges,
        out_shape=(
            message,
            message,
            jax.ShapeDtypeStruct((256, 512), BF16),
            jax.ShapeDtypeStruct((256, 128), F32),
            jax.ShapeDtypeStruct((108, 256), BF16),
        ),
        in_specs=[anywhere] * 2,
        out_specs=(vmem,) * 5,
        scratch_shapes=[pltpu.VMEM((2, 64, 4, 128), BF16), pltpu.SemaphoreType.DMA((2, 5))],
        compiler_params=pltpu.CompilerParams(vmem_limit_bytes=8 * 2**20),
        name="edges",
    )(inputs[0], inputs[-1])
    pairs = [(i, i ^ 1) for i in range(count)]
    others = [(i, i + 1) for i in range(1, count - 1, 2)] + [(i + 1, i) for i in range(1, count - 1, 2)]
    from_other = lax.ppermute(to_other, space, others)
    from_pair = lax.ppermute(to_pair, space, pairs)
    shapes = (
        ((256, 256), BF16),
        ((256, 1152), BF16),
        ((384, 768), BF16),
        ((256, 128), F32),
        ((256, 128), F32),
        ((4, 256, 128), BF16),
        ((8, 160, 128), BF16),
        ((2, 4, 256, 128), BF16),
        ((2, 384, 128), BF16),
    )
    own = pl.pallas_call(
        own_kernel,
        out_shape=tuple(jax.ShapeDtypeStruct(*shape) for shape in shapes),
        in_specs=[anywhere] * 6 + [vmem] * 2,
        out_specs=(vmem,) * len(shapes),
        scratch_shapes=[
            *(pltpu.VMEM(x.shape, x.dtype) for x in inputs),
            pltpu.VMEM((16, 128), F32),
            pltpu.VMEM((8 * 128 + 8, 128), F32),
            pltpu.VMEM((1040, 128), F32),
            pltpu.VMEM((64, 1024), F32),
            pltpu.SemaphoreType.DMA((6,)),
        ],
        compiler_params=pltpu.CompilerParams(vmem_limit_bytes=16 * 2**20),
        cost_estimate=pl.CostEstimate(flops=500_000_000, bytes_accessed=4_000_000, transcendentals=0),
        name="own_planes",
    )(*inputs, split, spread)

    def kernel(*refs):
        layers_kernel(
            *refs,
            space=space,
            last=count - 1,
            scale_first=1.0 / math.sqrt(cells),
            scale_second=1.0 / math.sqrt(cells / 8.0),
        )

    act, packed = pl.pallas_call(
        kernel,
        out_shape=(
            jax.ShapeDtypeStruct((64, 16, 128), BF16),
            jax.ShapeDtypeStruct((8, 64, 128), BF16),
        ),
        in_specs=[vmem] * (4 + len(shapes)),
        out_specs=(anywhere, vmem),
        scratch_shapes=[
            pltpu.VMEM((2, HALO * 128 + 8, 128), F32),
            pltpu.VMEM((HALO, 160, 128), BF16),
            pltpu.VMEM((HALO, 160, 128), BF16),
            pltpu.VMEM((264, 128), F32),
            pltpu.VMEM((8, 384, 128), BF16),
            pltpu.VMEM((2, 4, 256, 128), BF16),
            pltpu.VMEM((6 * 256, 128), BF16),
            pltpu.VMEM((1040, 128), F32),
            pltpu.VMEM((64, 16, 128), BF16),
            pltpu.SemaphoreType.DMA,
        ],
        compiler_params=pltpu.CompilerParams(vmem_limit_bytes=32 * 2**20),
        cost_estimate=pl.CostEstimate(flops=2_500_000_000, bytes_accessed=4_000_000, transcendentals=0),
        name="layers",
    )(from_other, from_pair, split, compact, *own)
    return act.reshape(1, 64, 4, 4, 128), packed


def solution(mesh):
    dp, space = mesh.shape["dp"], mesh.shape["space"]
    split = Mesh(mesh.devices.reshape((2,) * 9), BITS)

    def on_device(volume, w1, b1, w2, b2, cotangent):
        cells = float(math.prod(volume.shape[2:]) * dp * space)
        act, packed = local_step(volume, w1, b1, w2, b2, cotangent, SPACE, space, cells)
        total = sum_everywhere(packed)
        gw1, gb1, gw2, gb2 = pl.pallas_call(
            unpack_kernel,
            out_shape=(
                jax.ShapeDtypeStruct((32, 108), F32),
                jax.ShapeDtypeStruct((1, 32), F32),
                jax.ShapeDtypeStruct((64, 864), F32),
                jax.ShapeDtypeStruct((1, 64), F32),
            ),
            in_specs=[pl.BlockSpec(memory_space=pltpu.VMEM)],
            out_specs=(pl.BlockSpec(memory_space=pl.ANY),) * 4,
            scratch_shapes=[
                pltpu.VMEM((32, 108), F32),
                pltpu.VMEM((1, 32), F32),
                pltpu.VMEM((64, 864), F32),
                pltpu.VMEM((1, 64), F32),
                pltpu.SemaphoreType.DMA((7,)),
            ],
            compiler_params=pltpu.CompilerParams(vmem_limit_bytes=8 * 2**20),
            name="unpack",
        )(total)
        return act, gw1, gb1[0], gw2, gb2[0]

    shared = P(DP, None, SPACE, None, None)
    return jax.shard_map(
        on_device,
        mesh=split,
        in_specs=(shared, P(), P(), P(), P(), shared),
        out_specs=(shared, P(), P(), P(), P()),
        check_vma=False,
    )
```

```python
import math

import jax
import jax.numpy as jnp
import numpy as np
from jax import lax
from jax.experimental import pallas as pl
from jax.experimental.pallas import tpu as pltpu
from jax.sharding import Mesh, PartitionSpec as P

leak_slope = 0.3
F32, BF16 = jnp.float32, jnp.bfloat16
HALO = 5
NT = (((1,), (1,)), ((), ()))
BITS = ("z2", "z1", "z0", "y2", "x1", "x0", "y1", "y0", "c")
DP, SPACE = BITS[:4], BITS[4:]
CORES, Y, Z = ("x0", "x1", "c"), ("y0", "y1", "y2"), ("z0", "z1", "z2")


def edges_kernel(
    space, vol_hbm, cot_hbm, pair_ref, other_ref, split_ref, compact_ref, spread_ref, cot_s, sems
):
    second = lax.axis_index(space) % 2
    copies = []
    for side, ref, high in ((0, other_ref, second), (1, pair_ref, 1 - second)):
        copies.append(pltpu.make_async_copy(cot_hbm.at[:, high * 3], cot_s.at[side], sems.at[side, 4]))
        for c in range(4):
            source = vol_hbm.at[c, pl.ds(high * (8 - HALO), HALO)]
            copies.append(pltpu.make_async_copy(source, ref.at[pl.ds(c * HALO, HALO)], sems.at[side, c]))
    for copy in copies:
        copy.start()

    z = lax.broadcasted_iota(jnp.int32, (256, 128), 0)
    k = lax.broadcasted_iota(jnp.int32, (256, 128), 1)
    for dz in range(4):
        split_ref[:, dz * 128 : (dz + 1) * 128] = jnp.where(z == 2 * k - 1 + dz, 1.0, 0.0).astype(BF16)
    base = k // 36 * 64 + k // 12 % 3 * 16 + k % 12
    compact_ref[...] = jnp.where((z == base) & (k < 108), 1.0, 0.0)
    row = lax.broadcasted_iota(jnp.int32, (108, 256), 0)
    column = lax.broadcasted_iota(jnp.int32, (108, 256), 1)
    base = row // 36 * 64 + row // 12 % 3 * 16 + row % 12
    spread_ref[...] = jnp.where(column == base, 1.0, 0.0).astype(BF16)

    for copy in copies:
        copy.wait()
    for side, ref in ((0, other_ref), (1, pair_ref)):
        rows = cot_s[side].astype(F32).reshape(256, 128)
        rows = jnp.concatenate([rows[:128], rows[128:]], axis=1)
        ref[4 * HALO : 4 * HALO + 16] = rows.astype(BF16).reshape(16, 8, 256)


def add_kernel(parts_ref, out_ref):
    total = jnp.sum(parts_ref[...].astype(F32), axis=0).astype(BF16)
    for i in range(out_ref.shape[0]):
        out_ref[i] = total


def in_hbm(x):
    return pltpu.with_memory_space_constraint(x, pltpu.HBM)


def cell_shift(s):
    return (s // 2 % 2) * 64 + (s % 2) * 16 + (s // 4) * 4


def split_phases(rows, split, count, fine, win):
    parts = jnp.dot(rows, split, preferred_element_type=F32)
    for c in range(4):
        for x in range(count):
            for dz in range(4):
                fine[pl.ds(x * 128 + dz * 32 + c * 8, 8), :] = parts[
                    (c * count + x) * 8 : (c * count + x + 1) * 8, dz * 128 : (dz + 1) * 128
                ]
    for x in range(count):
        win[x, 0:16, :] = jnp.zeros((16, 128), BF16)
        win[x, 144:160, :] = jnp.zeros((16, 128), BF16)
        for y in range(8):
            win[x, (y + 1) * 16 : (y + 2) * 16, :] = fine[pl.ds(x * 128 + y, 16, stride=8), :].astype(BF16)


def window(planes, y):
    return jnp.concatenate([ref[x, 32 * y : 32 * y + 64, :] for ref, x in planes], axis=0)


def first_layer(planes, w1, bias, keep_pre, keep_pooled, mask):
    lane = lax.broadcasted_iota(jnp.int32, (32, 128), 1)
    for y0 in (0, 2):
        both = jnp.concatenate([window(planes, y0), window(planes, y0 + 1)], axis=1)
        pre = jnp.dot(w1, both, preferred_element_type=F32) + bias
        if keep_pre is not None:
            for i in range(2):
                keep_pre[y0 + i] = pre[:, i * 128 : (i + 1) * 128].astype(BF16)
        act = jnp.maximum(pre, leak_slope * pre)
        total = act[0:32]
        for s in range(1, 8):
            total = total + act[s * 32 : (s + 1) * 32]
        total = mask(total * 0.125)
        for i in range(2):
            pooled = total[:, i * 128 : (i + 1) * 128]
            at = (y0 + i) * 96
            keep_pooled[at : at + 32, :] = jnp.where(lane == 0, 0.0, pltpu.roll(pooled, 1, 1)).astype(BF16)
            keep_pooled[at + 32 : at + 64, :] = pooled.astype(BF16)
            keep_pooled[at + 64 : at + 96, :] = jnp.where(lane == 127, 0.0, pltpu.roll(pooled, 127, 1)).astype(BF16)


def own_kernel(
    w1_hbm, b1_hbm, b2_hbm, w2_hbm, vol_ref, cot_ref, split_ref, spread_ref,
    w1big_ref, wexp_ref, wt_ref, b1_ref, b2_ref, cot_out, win, pre_out, pooled_out,
    w1_ref, b1_row, b2_row, w2_ref, rows8, fine, cot_s, w2_pad, sems,
):
    sources, targets = (w1_hbm, b1_hbm, b2_hbm, w2_hbm), (w1_ref, b1_row, b2_row, w2_ref)
    copies = [pltpu.make_async_copy(x, y, sems.at[i]) for i, (x, y) in enumerate(zip(sources, targets))]
    for copy in copies:
        copy.start()
    rows8[...] = jnp.zeros((16, 128), F32)
    w2_pad[...] = jnp.zeros((64, 1024), F32)
    rows = vol_ref[...].astype(F32).reshape(256, 256).astype(BF16)
    split_phases(rows, split_ref[...], 8, fine, win)
    cot_s[0:1024, :] = cot_ref[...].astype(F32).reshape(1024, 128)
    for p in range(4):
        for y in range(4):
            cot_out[p, y * 64 : (y + 1) * 64, :] = cot_s[pl.ds(p * 4 + y, 64, stride=16), :].astype(BF16)

    for copy in copies:
        copy.wait()
    wide = jnp.dot(w1_ref[...], spread_ref[...], preferred_element_type=F32)
    for s in range(8):
        shift = cell_shift(s)
        moved = pltpu.roll(wide, shift, 1) if shift else wide
        w1big_ref[s * 32 : (s + 1) * 32, :] = moved.astype(BF16)
    rows8[0:1, 0:32] = b1_row[...]
    rows8[8:9, 0:64] = b2_row[...]
    b1 = jnp.broadcast_to(rows8[0:1, :], (128, 128)).T[:32]
    b1_ref[...] = jnp.concatenate([b1] * 8, axis=0)
    b2 = jnp.broadcast_to(rows8[8:9, :], (128, 128)).T[:64]
    b2_ref[...] = jnp.concatenate([b2] * 4, axis=0)
    bias = b1_ref[...]
    bias = jnp.concatenate([bias, bias], axis=1)
    for i in range(2):
        planes = [(win, 1 + 2 * i + dx) for dx in range(4)]
        first_layer(planes, w1big_ref[...], bias, pre_out.at[i], pooled_out.at[i], lambda v: v)

    w2_pad[:, 0:864] = w2_ref[...].astype(F32)
    lane = lax.broadcasted_iota(jnp.int32, (64, 512), 1)
    for dx in range(3):
        start = dx * 288 // 128 * 128
        taps = w2_pad[:, start : start + 512]
        rows = []
        for y in range(4):
            at = 96 * (y - 1)
            shift = (at - (dx * 288 - start)) % 512
            moved = pltpu.roll(taps, shift, 1) if shift else taps
            rows.append(jnp.where((lane >= max(at, 0)) & (lane < min(at + 288, 384)), moved, 0.0)[:, :384])
        for pair in range(2):
            block = jnp.concatenate(rows[2 * pair : 2 * pair + 2], axis=0)
            wexp_ref[pair * 128 : (pair + 1) * 128, dx * 384 : (dx + 1) * 384] = block.astype(BF16)
            col = (2 - dx) * 256 + pair * 128
            wt_ref[:, col : col + 128] = block.T.astype(BF16)


def layers_kernel(
    other_ref, pair_ref,
    split_ref, compact_ref, w1_ref, wexp_ref, wt_ref, b1_ref, b2_ref, cot_ref, win, pre_own, pooled_own,
    act_ref, grad_ref,
    fine, win_low, win_high, cot_s, ps, pre_s, g2s, act_s, act_out, sem,
    *, space, last, scale_first, scale_second,
):
    place = lax.axis_index(space)
    second = place % 2

    def side(low, start, stop):
        first, other = (other_ref, pair_ref) if low else (pair_ref, other_ref)
        return jnp.where(second == 0, first[start:stop].astype(F32), other[start:stop].astype(F32))

    for low, target in ((True, win_low), (False, win_high)):
        rows = side(low, 0, 4 * HALO).reshape(160, 256).astype(BF16)
        split_phases(rows, split_ref[...], HALO, fine.at[1 - low], target)

    def plane(x):
        if x < HALO:
            return win_low, x
        if x < HALO + 8:
            return win, x - HALO
        return win_high, x - HALO - 8

    bias1 = b1_ref[...]
    bias1 = jnp.concatenate([bias1, bias1], axis=1)
    bias2 = b2_ref[...]
    bias2 = jnp.concatenate([bias2, bias2], axis=1)
    for q in (0, 1, 2, 5, 6, 7):
        keep = pre_s.at[0] if q == 2 else pre_s.at[1] if q == 5 else None
        if q < 2:
            mask = lambda v: jnp.where(place > 0, v, 0.0)
        elif q > 5:
            mask = lambda v: jnp.where(place < last, v, 0.0)
        else:
            mask = lambda v: v
        first_layer([plane(2 * q + dx) for dx in range(4)], w1_ref[...], bias1, keep, ps.at[q], mask)

    def pooled(q):
        return pooled_own[q - 3] if q in (3, 4) else ps[q]

    def three(r):
        return jnp.concatenate([pooled(r), pooled(r + 1), pooled(r + 2)], axis=0)

    both = jnp.concatenate([three(r) for r in range(6)], axis=1)
    pre = jnp.dot(wexp_ref[...], both, preferred_element_type=F32) + jnp.concatenate([bias2] * 3, axis=1)
    act = jnp.maximum(pre, leak_slope * pre)
    for r in range(6):
        if 1 <= r <= 4:
            cot = cot_ref[r - 1].astype(F32)
            for y in range(4):
                act_s[pl.ds((r - 1) * 4 + y, 64, stride=16), :] = act[
                    y * 64 : (y + 1) * 64, r * 128 : (r + 1) * 128
                ]
        else:
            sent = side(r == 0, 4 * HALO, 4 * HALO + 16).reshape(128, 256)
            cot_s[0:128, :] = sent[:, 0:128]
            cot_s[128:256, :] = sent[:, 128:256]
            cot = jnp.concatenate([cot_s[pl.ds(y, 64, stride=4), :] for y in range(4)], axis=0)
        own = pre[:, r * 128 : (r + 1) * 128]
        g2s[r * 256 : (r + 1) * 256, :] = jnp.where(own > 0, cot, leak_slope * cot).astype(BF16)
    act_out[...] = act_s[0:1024, :].reshape(64, 16, 128).astype(BF16)
    copy = pltpu.make_async_copy(act_out, act_ref, sem)
    copy.start()

    lane = lax.broadcasted_iota(jnp.int32, (32, 128), 1)
    ones = jnp.ones((16, 512), BF16)
    all_cells, all_cols = [], []
    q = jnp.dot(
        wt_ref[...],
        jnp.concatenate([g2s[p * 256 : (p + 3) * 256, :] for p in range(4)], axis=1),
        preferred_element_type=F32,
    )
    for p in range(4):
        pre_p = pre_own.at[p - 1] if p in (1, 2) else pre_s.at[p // 3]
        cells = []
        for y in range(4):
            taps = q[y * 96 : (y + 1) * 96, p * 128 : (p + 1) * 128] * 0.125
            g = (
                jnp.where(lane == 127, 0.0, pltpu.roll(taps[0:32], 127, 1))
                + taps[32:64]
                + jnp.where(lane == 0, 0.0, pltpu.roll(taps[64:96], 1, 1))
            )
            low = leak_slope * g
            pre = pre_p[y].astype(F32)
            cells.append(
                jnp.concatenate(
                    [jnp.where(pre[s * 32 : (s + 1) * 32] > 0, g, low) for s in range(8)], axis=0
                ).astype(BF16)
            )
        planes = [plane(2 * (p + 2) + dx) for dx in range(4)]
        cols = jnp.concatenate([window(planes, y) for y in range(4)], axis=1)
        cols = jnp.concatenate([cols, ones], axis=0)
        all_cells.append(jnp.concatenate(cells, axis=1))
        all_cols.append(cols)
    m1 = lax.dot_general(
        jnp.concatenate(all_cells, axis=1), jnp.concatenate(all_cols, axis=1), NT, preferred_element_type=F32
    )

    lane96 = lax.broadcasted_iota(jnp.int32, (96, 128), 1)
    grads = jnp.concatenate([g2s[(p + 1) * 256 : (p + 2) * 256, :] for p in range(4)], axis=1)
    folded = []
    cols = [jnp.concatenate([pooled(p + 1 + dx) for p in range(4)], axis=1) for dx in range(3)]
    tt = lax.dot_general(jnp.concatenate(cols + [ones], axis=0), grads, NT, preferred_element_type=F32)
    b2_grad = tt[1152:1160, 0:128] + tt[1152:1160, 128:256]
    for dx in range(3):
        t = tt[dx * 384 : (dx + 1) * 384]
        for dy in range(3):
            sums = []
            for parity in range(2):
                total = None
                for y in (parity, parity + 2):
                    yin = y + dy - 1
                    if 0 <= yin < 4:
                        piece = t[yin * 96 : (yin + 1) * 96, (y // 2) * 128 : (y // 2 + 1) * 128]
                        total = piece if total is None else total + piece
                sums.append(total)
            u = jnp.where(lane96 < 64, sums[0], sums[1])
            folded.append(u + pltpu.roll(u, 64, 1))
    folded = jnp.concatenate(folded + [jnp.zeros((160, 128), F32)], axis=0) * scale_second
    lane128 = lax.broadcasted_iota(jnp.int32, (128, 128), 1)
    for j in range(0, 8, 2):
        two = jnp.where(lane128 < 64, folded[j * 128 : (j + 1) * 128], folded[(j + 1) * 128 : (j + 2) * 128]).T
        grad_ref[j] = two[:64].astype(BF16)
        if j < 6:
            grad_ref[j + 1] = two[64:].astype(BF16)

    total = m1[0:32, 0:256]
    for s in range(1, 8):
        total = total + pltpu.roll(m1[s * 32 : (s + 1) * 32, 0:256], 256 - cell_shift(s), 1)
    w1_grad = jnp.dot(total, compact_ref[...], precision=lax.Precision.HIGHEST, preferred_element_type=F32)
    sums = m1[0:32, 256:257]
    for s in range(1, 8):
        sums = sums + m1[s * 32 : (s + 1) * 32, 256:257]
    b1_grad = jnp.concatenate([jnp.broadcast_to(sums, (32, 128)), jnp.zeros((96, 128), F32)], axis=0).T[:8]
    b2_grad = b2_grad + pltpu.roll(b2_grad, 64, 1)
    biases = jnp.concatenate([b1_grad * scale_first, b2_grad * scale_second], axis=0)
    grad_ref[7, 0:32, :] = (w1_grad * scale_first).astype(BF16)
    grad_ref[7, 32:48, :] = biases.astype(BF16)
    grad_ref[7, 48:64, :] = jnp.zeros((16, 128), BF16)
    copy.wait()


def unpack_kernel(total_ref, w1_ref, b1_ref, w2_ref, b2_ref, w1_s, b1_s, w2_s, b2_s, sems):
    rest = total_ref[7].astype(F32)
    w1_s[...] = rest[0:32, 0:108]
    b1_s[...] = rest[32:33, 0:32]
    b2_s[...] = rest[40:41, 0:64]
    copies = []

    def send(source, target):
        copies.append(pltpu.make_async_copy(source, target, sems.at[len(copies)]))
        copies[-1].start()

    send(w1_s, w1_ref)
    send(b1_s, b1_ref)
    send(b2_s, b2_ref)
    for i in range(0, 64, 16):
        for j in range(6):
            w2_s[i : i + 16, j * 128 : (j + 1) * 128] = total_ref[j, i : i + 16].astype(F32)
        w2_s[i : i + 16, 768:864] = total_ref[6, i : i + 16].astype(F32)[:, :96]
        send(w2_s.at[pl.ds(i, 16)], w2_ref.at[pl.ds(i, 16)])
    for copy in copies:
        copy.wait()


def sum_everywhere(packed):
    vmem = pl.BlockSpec(memory_space=pltpu.VMEM)
    for axes in (CORES, Y, Z):
        parts = lax.all_to_all(packed, axes, 0, 0, tiled=True)
        packed = pl.pallas_call(
            add_kernel,
            out_shape=jax.ShapeDtypeStruct(packed.shape, packed.dtype),
            in_specs=[vmem],
            out_specs=vmem,
            compiler_params=pltpu.CompilerParams(vmem_limit_bytes=8 * 2**20),
            name="add",
        )(parts)
    return lax.all_to_all(packed, CORES, 0, 0, tiled=True)


def local_step(volume, w1, b1, w2, b2, cotangent, space, count, cells):
    vol, cot = volume[0], cotangent[0]
    vmem, anywhere = pl.BlockSpec(memory_space=pltpu.VMEM), pl.BlockSpec(memory_space=pl.ANY)

    def edges(*refs):
        edges_kernel(space, *refs)

    weights = [in_hbm(x) for x in (w1, b1.reshape(1, 32), b2.reshape(1, 64), w2)]
    message = jax.ShapeDtypeStruct((4 * HALO + 16, 8, 256), BF16)
    to_pair, to_other, split, compact, spread = pl.pallas_call(
        edges,
        out_shape=(
            message,
            message,
            jax.ShapeDtypeStruct((256, 512), BF16),
            jax.ShapeDtypeStruct((256, 128), F32),
            jax.ShapeDtypeStruct((108, 256), BF16),
        ),
        in_specs=[anywhere] * 2,
        out_specs=(vmem,) * 5,
        scratch_shapes=[pltpu.VMEM((2, 64, 4, 128), BF16), pltpu.SemaphoreType.DMA((2, 5))],
        compiler_params=pltpu.CompilerParams(vmem_limit_bytes=8 * 2**20),
        name="edges",
    )(in_hbm(vol), in_hbm(cot))
    pairs = [(i, i ^ 1) for i in range(count)]
    others = [(i, i + 1) for i in range(1, count - 1, 2)] + [(i + 1, i) for i in range(1, count - 1, 2)]
    from_other = lax.ppermute(to_other, space, others)
    from_pair = lax.ppermute(to_pair, space, pairs)
    shapes = (
        ((256, 256), BF16),
        ((256, 1152), BF16),
        ((384, 768), BF16),
        ((256, 128), F32),
        ((256, 128), F32),
        ((4, 256, 128), BF16),
        ((8, 160, 128), BF16),
        ((2, 4, 256, 128), BF16),
        ((2, 384, 128), BF16),
    )
    own = pl.pallas_call(
        own_kernel,
        out_shape=tuple(jax.ShapeDtypeStruct(*shape) for shape in shapes),
        in_specs=[anywhere] * 4 + [vmem] * 4,
        out_specs=(vmem,) * len(shapes),
        scratch_shapes=[
            *(pltpu.VMEM(x.shape, x.dtype) for x in weights),
            pltpu.VMEM((16, 128), F32),
            pltpu.VMEM((8 * 128 + 8, 128), F32),
            pltpu.VMEM((1040, 128), F32),
            pltpu.VMEM((64, 1024), F32),
            pltpu.SemaphoreType.DMA((4,)),
        ],
        compiler_params=pltpu.CompilerParams(vmem_limit_bytes=16 * 2**20),
        cost_estimate=pl.CostEstimate(flops=500_000_000, bytes_accessed=4_000_000, transcendentals=0),
        name="own_planes",
    )(*weights, vol, cot, split, spread)

    def kernel(*refs):
        layers_kernel(
            *refs,
            space=space,
            last=count - 1,
            scale_first=1.0 / math.sqrt(cells),
            scale_second=1.0 / math.sqrt(cells / 8.0),
        )

    act, packed = pl.pallas_call(
        kernel,
        out_shape=(
            jax.ShapeDtypeStruct((64, 16, 128), BF16),
            jax.ShapeDtypeStruct((8, 64, 128), BF16),
        ),
        in_specs=[vmem] * (4 + len(shapes)),
        out_specs=(anywhere, vmem),
        scratch_shapes=[
            pltpu.VMEM((2, HALO * 128 + 8, 128), F32),
            pltpu.VMEM((HALO, 160, 128), BF16),
            pltpu.VMEM((HALO, 160, 128), BF16),
            pltpu.VMEM((264, 128), F32),
            pltpu.VMEM((8, 384, 128), BF16),
            pltpu.VMEM((2, 4, 256, 128), BF16),
            pltpu.VMEM((6 * 256, 128), BF16),
            pltpu.VMEM((1040, 128), F32),
            pltpu.VMEM((64, 16, 128), BF16),
            pltpu.SemaphoreType.DMA,
        ],
        compiler_params=pltpu.CompilerParams(vmem_limit_bytes=32 * 2**20),
        cost_estimate=pl.CostEstimate(flops=2_500_000_000, bytes_accessed=4_000_000, transcendentals=0),
        name="layers",
    )(from_other, from_pair, split, compact, *own)
    return act.reshape(1, 64, 4, 4, 128), packed


def solution(mesh):
    dp, space = mesh.shape["dp"], mesh.shape["space"]
    split = Mesh(mesh.devices.reshape((2,) * 9), BITS)

    def on_device(volume, w1, b1, w2, b2, cotangent):
        cells = float(math.prod(volume.shape[2:]) * dp * space)
        act, packed = local_step(volume, w1, b1, w2, b2, cotangent, SPACE, space, cells)
        total = sum_everywhere(packed)
        gw1, gb1, gw2, gb2 = pl.pallas_call(
            unpack_kernel,
            out_shape=(
                jax.ShapeDtypeStruct((32, 108), F32),
                jax.ShapeDtypeStruct((1, 32), F32),
                jax.ShapeDtypeStruct((64, 864), F32),
                jax.ShapeDtypeStruct((1, 64), F32),
            ),
            in_specs=[pl.BlockSpec(memory_space=pltpu.VMEM)],
            out_specs=(pl.BlockSpec(memory_space=pl.ANY),) * 4,
            scratch_shapes=[
                pltpu.VMEM((32, 108), F32),
                pltpu.VMEM((1, 32), F32),
                pltpu.VMEM((64, 864), F32),
                pltpu.VMEM((1, 64), F32),
                pltpu.SemaphoreType.DMA((7,)),
            ],
            compiler_params=pltpu.CompilerParams(vmem_limit_bytes=8 * 2**20),
            name="unpack",
        )(total)
        return act, gw1, gb1[0], gw2, gb2[0]

    shared = P(DP, None, SPACE, None, None)
    return jax.shard_map(
        on_device,
        mesh=split,
        in_specs=(shared, P(), P(), P(), P(), shared),
        out_specs=(shared, P(), P(), P(), P()),
        check_vma=False,
    )
```

```python
import math

import jax
import jax.numpy as jnp
import numpy as np
from jax import lax
from jax.experimental import pallas as pl
from jax.experimental.pallas import tpu as pltpu
from jax.sharding import Mesh, PartitionSpec as P

leak_slope = 0.3
F32, BF16 = jnp.float32, jnp.bfloat16
HALO = 5
NT = (((1,), (1,)), ((), ()))
BITS = ("z2", "z1", "z0", "y2", "x1", "x0", "y1", "y0", "c")
DP, SPACE = BITS[:4], BITS[4:]
CORES, Y, Z = ("x0", "x1", "c"), ("y0", "y1", "y2"), ("z0", "z1", "z2")


def edges_kernel(
    space, vol_hbm, cot_hbm, pair_ref, other_ref, split_ref, compact_ref, spread_ref, cot_s, sems
):
    second = lax.axis_index(space) % 2
    copies = []
    for side, ref, high in ((0, other_ref, second), (1, pair_ref, 1 - second)):
        copies.append(pltpu.make_async_copy(cot_hbm.at[:, high * 3], cot_s.at[side], sems.at[side, 4]))
        for c in range(4):
            source = vol_hbm.at[c, pl.ds(high * (8 - HALO), HALO)]
            copies.append(pltpu.make_async_copy(source, ref.at[pl.ds(c * HALO, HALO)], sems.at[side, c]))
    for copy in copies:
        copy.start()

    z = lax.broadcasted_iota(jnp.int32, (256, 128), 0)
    k = lax.broadcasted_iota(jnp.int32, (256, 128), 1)
    for dz in range(4):
        split_ref[:, dz * 128 : (dz + 1) * 128] = jnp.where(z == 2 * k - 1 + dz, 1.0, 0.0).astype(BF16)
    base = k // 36 * 64 + k // 12 % 3 * 16 + k % 12
    compact_ref[...] = jnp.where((z == base) & (k < 108), 1.0, 0.0)
    row = lax.broadcasted_iota(jnp.int32, (108, 256), 0)
    column = lax.broadcasted_iota(jnp.int32, (108, 256), 1)
    base = row // 36 * 64 + row // 12 % 3 * 16 + row % 12
    spread_ref[...] = jnp.where(column == base, 1.0, 0.0).astype(BF16)

    for copy in copies:
        copy.wait()
    for side, ref in ((0, other_ref), (1, pair_ref)):
        rows = cot_s[side].astype(F32).reshape(256, 128)
        rows = jnp.concatenate([rows[:128], rows[128:]], axis=1)
        ref[4 * HALO : 4 * HALO + 16] = rows.astype(BF16).reshape(16, 8, 256)


def add_kernel(parts_ref, out_ref):
    total = jnp.sum(parts_ref[...].astype(F32), axis=0).astype(BF16)
    for i in range(out_ref.shape[0]):
        out_ref[i] = total


def in_hbm(x):
    return pltpu.with_memory_space_constraint(x, pltpu.HBM)


def cell_shift(s):
    return (s // 2 % 2) * 64 + (s % 2) * 16 + (s // 4) * 4


def split_phases(rows, split, count, fine, win):
    parts = jnp.dot(rows, split, preferred_element_type=F32)
    for c in range(4):
        for x in range(count):
            for dz in range(4):
                fine[pl.ds(x * 128 + dz * 32 + c * 8, 8), :] = parts[
                    (c * count + x) * 8 : (c * count + x + 1) * 8, dz * 128 : (dz + 1) * 128
                ]
    for x in range(count):
        win[x, 0:16, :] = jnp.zeros((16, 128), BF16)
        win[x, 144:160, :] = jnp.zeros((16, 128), BF16)
        for y in range(8):
            win[x, (y + 1) * 16 : (y + 2) * 16, :] = fine[pl.ds(x * 128 + y, 16, stride=8), :].astype(BF16)


def window(planes, y):
    return jnp.concatenate([ref[x, 32 * y : 32 * y + 64, :] for ref, x in planes], axis=0)


def first_layer(planes, w1, bias, keep_pre, keep_pooled, mask):
    lane = lax.broadcasted_iota(jnp.int32, (32, 128), 1)
    for y0 in (0, 2):
        both = jnp.concatenate([window(planes, y0), window(planes, y0 + 1)], axis=1)
        pre = jnp.dot(w1, both, preferred_element_type=F32) + bias
        if keep_pre is not None:
            for i in range(2):
                keep_pre[y0 + i] = pre[:, i * 128 : (i + 1) * 128].astype(BF16)
        act = jnp.maximum(pre, leak_slope * pre)
        total = act[0:32]
        for s in range(1, 8):
            total = total + act[s * 32 : (s + 1) * 32]
        total = mask(total * 0.125)
        for i in range(2):
            pooled = total[:, i * 128 : (i + 1) * 128]
            at = (y0 + i) * 96
            keep_pooled[at : at + 32, :] = jnp.where(lane == 0, 0.0, pltpu.roll(pooled, 1, 1)).astype(BF16)
            keep_pooled[at + 32 : at + 64, :] = pooled.astype(BF16)
            keep_pooled[at + 64 : at + 96, :] = jnp.where(lane == 127, 0.0, pltpu.roll(pooled, 127, 1)).astype(BF16)


def own_kernel(
    w1_hbm, b1_hbm, b2_hbm, w2_hbm, vol_ref, cot_ref, split_ref, spread_ref,
    w1big_ref, wexp_ref, wt_ref, b1_ref, b2_ref, cot_out, win, pre_out, pooled_out,
    w1_ref, b1_row, b2_row, w2_ref, rows8, fine, cot_s, w2_pad, sems,
):
    sources, targets = (w1_hbm, b1_hbm, b2_hbm, w2_hbm), (w1_ref, b1_row, b2_row, w2_ref)
    copies = [pltpu.make_async_copy(x, y, sems.at[i]) for i, (x, y) in enumerate(zip(sources, targets))]
    for copy in copies:
        copy.start()
    rows8[...] = jnp.zeros((16, 128), F32)
    w2_pad[...] = jnp.zeros((64, 1024), F32)
    rows = vol_ref[...].astype(F32).reshape(256, 256).astype(BF16)
    split_phases(rows, split_ref[...], 8, fine, win)
    cot_s[0:1024, :] = cot_ref[...].astype(F32).reshape(1024, 128)
    for p in range(4):
        for y in range(4):
            cot_out[p, y * 64 : (y + 1) * 64, :] = cot_s[pl.ds(p * 4 + y, 64, stride=16), :].astype(BF16)

    for copy in copies:
        copy.wait()
    wide = jnp.dot(w1_ref[...], spread_ref[...], preferred_element_type=F32)
    for s in range(8):
        shift = cell_shift(s)
        moved = pltpu.roll(wide, shift, 1) if shift else wide
        w1big_ref[s * 32 : (s + 1) * 32, :] = moved.astype(BF16)
    rows8[0:1, 0:32] = b1_row[...]
    rows8[8:9, 0:64] = b2_row[...]
    b1 = jnp.broadcast_to(rows8[0:1, :], (128, 128)).T[:32]
    b1_ref[...] = jnp.concatenate([b1] * 8, axis=0)
    b2 = jnp.broadcast_to(rows8[8:9, :], (128, 128)).T[:64]
    b2_ref[...] = jnp.concatenate([b2] * 4, axis=0)
    bias = b1_ref[...]
    bias = jnp.concatenate([bias, bias], axis=1)
    for i in range(2):
        planes = [(win, 1 + 2 * i + dx) for dx in range(4)]
        first_layer(planes, w1big_ref[...], bias, pre_out.at[i], pooled_out.at[i], lambda v: v)

    w2_pad[:, 0:864] = w2_ref[...].astype(F32)
    lane = lax.broadcasted_iota(jnp.int32, (64, 512), 1)
    for dx in range(3):
        start = dx * 288 // 128 * 128
        taps = w2_pad[:, start : start + 512]
        rows = []
        for y in range(4):
            at = 96 * (y - 1)
            shift = (at - (dx * 288 - start)) % 512
            moved = pltpu.roll(taps, shift, 1) if shift else taps
            rows.append(jnp.where((lane >= max(at, 0)) & (lane < min(at + 288, 384)), moved, 0.0)[:, :384])
        for pair in range(2):
            block = jnp.concatenate(rows[2 * pair : 2 * pair + 2], axis=0)
            wexp_ref[pair * 128 : (pair + 1) * 128, dx * 384 : (dx + 1) * 384] = block.astype(BF16)
            col = (2 - dx) * 256 + pair * 128
            wt_ref[:, col : col + 128] = block.T.astype(BF16)


def layers_kernel(
    other_ref, pair_ref,
    split_ref, compact_ref, w1_ref, wexp_ref, wt_ref, b1_ref, b2_ref, cot_ref, win, pre_own, pooled_own,
    act_ref, grad_ref,
    fine, win_low, win_high, cot_s, ps, pre_s, g2s, act_s,
    *, space, last, scale_first, scale_second,
):
    place = lax.axis_index(space)
    second = place % 2

    def side(low, start, stop):
        first, other = (other_ref, pair_ref) if low else (pair_ref, other_ref)
        return jnp.where(second == 0, first[start:stop].astype(F32), other[start:stop].astype(F32))

    for low, target in ((True, win_low), (False, win_high)):
        rows = side(low, 0, 4 * HALO).reshape(160, 256).astype(BF16)
        split_phases(rows, split_ref[...], HALO, fine.at[1 - low], target)

    def plane(x):
        if x < HALO:
            return win_low, x
        if x < HALO + 8:
            return win, x - HALO
        return win_high, x - HALO - 8

    bias1 = b1_ref[...]
    bias1 = jnp.concatenate([bias1, bias1], axis=1)
    bias2 = b2_ref[...]
    bias2 = jnp.concatenate([bias2, bias2], axis=1)
    for q in (0, 1, 2, 5, 6, 7):
        keep = pre_s.at[0] if q == 2 else pre_s.at[1] if q == 5 else None
        if q < 2:
            mask = lambda v: jnp.where(place > 0, v, 0.0)
        elif q > 5:
            mask = lambda v: jnp.where(place < last, v, 0.0)
        else:
            mask = lambda v: v
        first_layer([plane(2 * q + dx) for dx in range(4)], w1_ref[...], bias1, keep, ps.at[q], mask)

    def pooled(q):
        return pooled_own[q - 3] if q in (3, 4) else ps[q]

    def three(r):
        return jnp.concatenate([pooled(r), pooled(r + 1), pooled(r + 2)], axis=0)

    both = jnp.concatenate([three(r) for r in range(6)], axis=1)
    pre = jnp.dot(wexp_ref[...], both, preferred_element_type=F32) + jnp.concatenate([bias2] * 3, axis=1)
    act = jnp.maximum(pre, leak_slope * pre)
    for r in range(6):
        if 1 <= r <= 4:
            cot = cot_ref[r - 1].astype(F32)
            for y in range(4):
                act_s[pl.ds((r - 1) * 4 + y, 64, stride=16), :] = act[
                    y * 64 : (y + 1) * 64, r * 128 : (r + 1) * 128
                ]
        else:
            sent = side(r == 0, 4 * HALO, 4 * HALO + 16).reshape(128, 256)
            cot_s[0:128, :] = sent[:, 0:128]
            cot_s[128:256, :] = sent[:, 128:256]
            cot = jnp.concatenate([cot_s[pl.ds(y, 64, stride=4), :] for y in range(4)], axis=0)
        own = pre[:, r * 128 : (r + 1) * 128]
        g2s[r * 256 : (r + 1) * 256, :] = jnp.where(own > 0, cot, leak_slope * cot).astype(BF16)
    act_ref[...] = act_s[0:1024, :].reshape(64, 16, 128).astype(BF16)

    lane = lax.broadcasted_iota(jnp.int32, (32, 128), 1)
    ones = jnp.ones((16, 512), BF16)
    all_cells, all_cols = [], []
    q = jnp.dot(
        wt_ref[...],
        jnp.concatenate([g2s[p * 256 : (p + 3) * 256, :] for p in range(4)], axis=1),
        preferred_element_type=F32,
    )
    for p in range(4):
        pre_p = pre_own.at[p - 1] if p in (1, 2) else pre_s.at[p // 3]
        cells = []
        for y in range(4):
            taps = q[y * 96 : (y + 1) * 96, p * 128 : (p + 1) * 128] * 0.125
            g = (
                jnp.where(lane == 127, 0.0, pltpu.roll(taps[0:32], 127, 1))
                + taps[32:64]
                + jnp.where(lane == 0, 0.0, pltpu.roll(taps[64:96], 1, 1))
            )
            low = leak_slope * g
            pre = pre_p[y].astype(F32)
            cells.append(
                jnp.concatenate(
                    [jnp.where(pre[s * 32 : (s + 1) * 32] > 0, g, low) for s in range(8)], axis=0
                ).astype(BF16)
            )
        planes = [plane(2 * (p + 2) + dx) for dx in range(4)]
        cols = jnp.concatenate([window(planes, y) for y in range(4)], axis=1)
        cols = jnp.concatenate([cols, ones], axis=0)
        all_cells.append(jnp.concatenate(cells, axis=1))
        all_cols.append(cols)
    m1 = lax.dot_general(
        jnp.concatenate(all_cells, axis=1), jnp.concatenate(all_cols, axis=1), NT, preferred_element_type=F32
    )

    lane96 = lax.broadcasted_iota(jnp.int32, (96, 128), 1)
    grads = jnp.concatenate([g2s[(p + 1) * 256 : (p + 2) * 256, :] for p in range(4)], axis=1)
    folded = []
    cols = [jnp.concatenate([pooled(p + 1 + dx) for p in range(4)], axis=1) for dx in range(3)]
    tt = lax.dot_general(jnp.concatenate(cols + [ones], axis=0), grads, NT, preferred_element_type=F32)
    b2_grad = tt[1152:1160, 0:128] + tt[1152:1160, 128:256]
    for dx in range(3):
        t = tt[dx * 384 : (dx + 1) * 384]
        for dy in range(3):
            sums = []
            for parity in range(2):
                total = None
                for y in (parity, parity + 2):
                    yin = y + dy - 1
                    if 0 <= yin < 4:
                        piece = t[yin * 96 : (yin + 1) * 96, (y // 2) * 128 : (y // 2 + 1) * 128]
                        total = piece if total is None else total + piece
                sums.append(total)
            u = jnp.where(lane96 < 64, sums[0], sums[1])
            folded.append(u + pltpu.roll(u, 64, 1))
    folded = jnp.concatenate(folded + [jnp.zeros((160, 128), F32)], axis=0) * scale_second
    lane128 = lax.broadcasted_iota(jnp.int32, (128, 128), 1)
    for j in range(0, 8, 2):
        two = jnp.where(lane128 < 64, folded[j * 128 : (j + 1) * 128], folded[(j + 1) * 128 : (j + 2) * 128]).T
        grad_ref[j] = two[:64].astype(BF16)
        if j < 6:
            grad_ref[j + 1] = two[64:].astype(BF16)

    total = m1[0:32, 0:256]
    for s in range(1, 8):
        total = total + pltpu.roll(m1[s * 32 : (s + 1) * 32, 0:256], 256 - cell_shift(s), 1)
    w1_grad = jnp.dot(total, compact_ref[...], precision=lax.Precision.HIGHEST, preferred_element_type=F32)
    sums = m1[0:32, 256:257]
    for s in range(1, 8):
        sums = sums + m1[s * 32 : (s + 1) * 32, 256:257]
    b1_grad = jnp.concatenate([jnp.broadcast_to(sums, (32, 128)), jnp.zeros((96, 128), F32)], axis=0).T[:8]
    b2_grad = b2_grad + pltpu.roll(b2_grad, 64, 1)
    biases = jnp.concatenate([b1_grad * scale_first, b2_grad * scale_second], axis=0)
    grad_ref[7, 0:32, :] = (w1_grad * scale_first).astype(BF16)
    grad_ref[7, 32:48, :] = biases.astype(BF16)
    grad_ref[7, 48:64, :] = jnp.zeros((16, 128), BF16)


def finish_kernel(
    total_ref, act_s, w1_ref, b1_ref, w2_ref, b2_ref, act_ref, w1_s, b1_s, w2_s, b2_s, sems
):
    copies = []

    def send(source, target):
        copies.append(pltpu.make_async_copy(source, target, sems.at[len(copies)]))
        copies[-1].start()

    send(act_s, act_ref)
    rest = total_ref[7].astype(F32)
    w1_s[...] = rest[0:32, 0:108]
    b1_s[...] = rest[32:33, 0:32]
    b2_s[...] = rest[40:41, 0:64]
    send(w1_s, w1_ref)
    send(b1_s, b1_ref)
    send(b2_s, b2_ref)
    for i in range(0, 64, 16):
        for j in range(6):
            w2_s[i : i + 16, j * 128 : (j + 1) * 128] = total_ref[j, i : i + 16].astype(F32)
        w2_s[i : i + 16, 768:864] = total_ref[6, i : i + 16].astype(F32)[:, :96]
        send(w2_s.at[pl.ds(i, 16)], w2_ref.at[pl.ds(i, 16)])
    for copy in copies:
        copy.wait()


def sum_everywhere(packed):
    vmem = pl.BlockSpec(memory_space=pltpu.VMEM)
    for axes in (CORES, Y, Z):
        parts = lax.all_to_all(packed, axes, 0, 0, tiled=True)
        packed = pl.pallas_call(
            add_kernel,
            out_shape=jax.ShapeDtypeStruct(packed.shape, packed.dtype),
            in_specs=[vmem],
            out_specs=vmem,
            compiler_params=pltpu.CompilerParams(vmem_limit_bytes=8 * 2**20),
            name="add",
        )(parts)
    return lax.all_to_all(packed, CORES, 0, 0, tiled=True)


def local_step(volume, w1, b1, w2, b2, cotangent, space, count, cells):
    vol, cot = volume[0], cotangent[0]
    vmem, anywhere = pl.BlockSpec(memory_space=pltpu.VMEM), pl.BlockSpec(memory_space=pl.ANY)

    def edges(*refs):
        edges_kernel(space, *refs)

    weights = [in_hbm(x) for x in (w1, b1.reshape(1, 32), b2.reshape(1, 64), w2)]
    message = jax.ShapeDtypeStruct((4 * HALO + 16, 8, 256), BF16)
    to_pair, to_other, split, compact, spread = pl.pallas_call(
        edges,
        out_shape=(
            message,
            message,
            jax.ShapeDtypeStruct((256, 512), BF16),
            jax.ShapeDtypeStruct((256, 128), F32),
            jax.ShapeDtypeStruct((108, 256), BF16),
        ),
        in_specs=[anywhere] * 2,
        out_specs=(vmem,) * 5,
        scratch_shapes=[pltpu.VMEM((2, 64, 4, 128), BF16), pltpu.SemaphoreType.DMA((2, 5))],
        compiler_params=pltpu.CompilerParams(vmem_limit_bytes=8 * 2**20),
        name="edges",
    )(in_hbm(vol), in_hbm(cot))
    pairs = [(i, i ^ 1) for i in range(count)]
    others = [(i, i + 1) for i in range(1, count - 1, 2)] + [(i + 1, i) for i in range(1, count - 1, 2)]
    from_other = lax.ppermute(to_other, space, others)
    from_pair = lax.ppermute(to_pair, space, pairs)
    shapes = (
        ((256, 256), BF16),
        ((256, 1152), BF16),
        ((384, 768), BF16),
        ((256, 128), F32),
        ((256, 128), F32),
        ((4, 256, 128), BF16),
        ((8, 160, 128), BF16),
        ((2, 4, 256, 128), BF16),
        ((2, 384, 128), BF16),
    )
    own = pl.pallas_call(
        own_kernel,
        out_shape=tuple(jax.ShapeDtypeStruct(*shape) for shape in shapes),
        in_specs=[anywhere] * 4 + [vmem] * 4,
        out_specs=(vmem,) * len(shapes),
        scratch_shapes=[
            *(pltpu.VMEM(x.shape, x.dtype) for x in weights),
            pltpu.VMEM((16, 128), F32),
            pltpu.VMEM((8 * 128 + 8, 128), F32),
            pltpu.VMEM((1040, 128), F32),
            pltpu.VMEM((64, 1024), F32),
            pltpu.SemaphoreType.DMA((4,)),
        ],
        compiler_params=pltpu.CompilerParams(vmem_limit_bytes=16 * 2**20),
        cost_estimate=pl.CostEstimate(flops=500_000_000, bytes_accessed=4_000_000, transcendentals=0),
        name="own_planes",
    )(*weights, vol, cot, split, spread)

    def kernel(*refs):
        layers_kernel(
            *refs,
            space=space,
            last=count - 1,
            scale_first=1.0 / math.sqrt(cells),
            scale_second=1.0 / math.sqrt(cells / 8.0),
        )

    act, packed = pl.pallas_call(
        kernel,
        out_shape=(
            jax.ShapeDtypeStruct((64, 16, 128), BF16),
            jax.ShapeDtypeStruct((8, 64, 128), BF16),
        ),
        in_specs=[vmem] * (4 + len(shapes)),
        out_specs=(vmem, vmem),
        scratch_shapes=[
            pltpu.VMEM((2, HALO * 128 + 8, 128), F32),
            pltpu.VMEM((HALO, 160, 128), BF16),
            pltpu.VMEM((HALO, 160, 128), BF16),
            pltpu.VMEM((264, 128), F32),
            pltpu.VMEM((8, 384, 128), BF16),
            pltpu.VMEM((2, 4, 256, 128), BF16),
            pltpu.VMEM((6 * 256, 128), BF16),
            pltpu.VMEM((1040, 128), F32),
        ],
        compiler_params=pltpu.CompilerParams(vmem_limit_bytes=32 * 2**20),
        cost_estimate=pl.CostEstimate(flops=2_500_000_000, bytes_accessed=4_000_000, transcendentals=0),
        name="layers",
    )(from_other, from_pair, split, compact, *own)
    return act, packed


def solution(mesh):
    dp, space = mesh.shape["dp"], mesh.shape["space"]
    split = Mesh(mesh.devices.reshape((2,) * 9), BITS)

    def on_device(volume, w1, b1, w2, b2, cotangent):
        cells = float(math.prod(volume.shape[2:]) * dp * space)
        act, packed = local_step(volume, w1, b1, w2, b2, cotangent, SPACE, space, cells)
        total = sum_everywhere(packed)
        gw1, gb1, gw2, gb2, act = pl.pallas_call(
            finish_kernel,
            out_shape=(
                jax.ShapeDtypeStruct((32, 108), F32),
                jax.ShapeDtypeStruct((1, 32), F32),
                jax.ShapeDtypeStruct((64, 864), F32),
                jax.ShapeDtypeStruct((1, 64), F32),
                jax.ShapeDtypeStruct((64, 16, 128), BF16),
            ),
            in_specs=[pl.BlockSpec(memory_space=pltpu.VMEM)] * 2,
            out_specs=(pl.BlockSpec(memory_space=pl.ANY),) * 5,
            scratch_shapes=[
                pltpu.VMEM((32, 108), F32),
                pltpu.VMEM((1, 32), F32),
                pltpu.VMEM((64, 864), F32),
                pltpu.VMEM((1, 64), F32),
                pltpu.SemaphoreType.DMA((8,)),
            ],
            compiler_params=pltpu.CompilerParams(vmem_limit_bytes=8 * 2**20),
            name="finish",
        )(total, act)
        return act.reshape(1, 64, 4, 4, 128), gw1, gb1[0], gw2, gb2[0]

    shared = P(DP, None, SPACE, None, None)
    return jax.shard_map(
        on_device,
        mesh=split,
        in_specs=(shared, P(), P(), P(), P(), shared),
        out_specs=(shared, P(), P(), P(), P()),
        check_vma=False,
    )
```
